256 devices in a mesh: dp: 2 (over core), row: 8 (over y, x_hi), col: 16 (over x_lo, z).
Axes of the slice: x: 4 (x_hi: 2, x_lo: 2; x = x_hi * 2 + x_lo), y: 4, z: 8, core: 2. Of those that a mesh axis runs over, the one named last changes fastest.
Arguments:
- tokens: bfloat16 [4096, 4096], P(('dp', 'col'), 'row'), may hold values from -6 to 6
- cotangent: bfloat16 [4096, 4096], P(('dp', 'col'), 'row'), may hold values from -6 to 6
- gate_blocks: bfloat16 [128, 4, 128, 128], P(('row', 'col')), may hold values from -0.3125 to 0.3125
- up_blocks: bfloat16 [128, 4, 128, 128], P(('row', 'col')), may hold values from -0.3125 to 0.3125
- down_blocks: bfloat16 [128, 4, 128, 128], P(('row', 'col')), may hold values from -0.15625 to 0.15625
- gate_index: int32 [128, 4], replicated, may hold values from 0 to 32, as said below
- up_index: int32 [128, 4], replicated, may hold values from 0 to 32, as said below
- down_index: int32 [128, 4], replicated, may hold values from 0 to 32, as said below
Outputs:
- block_output: bfloat16 [4096, 4096], P(('dp', 'col'), 'row')
- input_grad: bfloat16 [4096, 4096], P(('dp', 'col'), 'row')
- gate_grad: float32 [128, 4, 128, 128], P(('row', 'col'))
- up_grad: float32 [128, 4, 128, 128], P(('row', 'col'))
- down_grad: float32 [128, 4, 128, 128], P(('row', 'col'))
The draws below stay inside these ranges and needn't reach their ends.
Inputs may be any that keep to these rules, and one draw needn't show every extreme that they name: `gate_index`: in each panel's row the used slots come first and hold distinct block numbers in ascending order; the other slots hold 32. Each panel uses 2 to 4 slots, and some panel uses all 4. `up_index`: as for gate_index. `down_index`: as for gate_index.
All inputs are finite; a program needn't handle non-finite values.
Results may differ from the reference program's by a relative error of at most 0.023.
Values may be sent and summed in bfloat16 or wider, within the bound.
A program may use at most 128 MiB of HBM per device.

```python
import jax
import jax.numpy as jnp
from jax import lax

D = 4096
FF = 16384
BLK = 128
SLOTS = 4
TOK_GRP = 128
NPANEL = 128
TOKENS = 4096
N_ROW = 8


def pattern(base_key):
    panel_total = FF // BLK
    block_count = D // BLK
    first_key, second_key, third_key = jax.random.split(base_key, 3)
    used = jax.random.randint(first_key, (panel_total,), 2, SLOTS + 1)
    chosen = jax.random.randint(second_key, (), 0, panel_total)
    used = jnp.where(jnp.arange(panel_total) == chosen, SLOTS, used)
    scores = jax.random.randint(third_key, (panel_total, block_count), 0, 1 << 20) * block_count
    scores = scores + jnp.arange(block_count, dtype=jnp.int32)[None, :]
    ordering = jnp.argsort(scores, axis=1)[:, :SLOTS].astype(jnp.int32)
    live = jnp.arange(SLOTS)[None, :] < used[:, None]
    return jnp.sort(jnp.where(live, ordering, block_count), axis=1).astype(jnp.int32)


def draw_gate_index(base_key, part_index):
    base_key = jax.random.fold_in(base_key, 11)
    return pattern(base_key)


def draw_up_index(base_key, part_index):
    base_key = jax.random.fold_in(base_key, 23)
    return pattern(base_key)


def draw_down_index(base_key, part_index):
    base_key = jax.random.fold_in(base_key, 37)
    return pattern(base_key)


def steps_of(rng, shape, cuts, low, largest):
    level = 1.0
    for position, parts in cuts:
        heights = jax.random.uniform(jax.random.fold_in(jax.random.fold_in(rng, 6), position), (parts,), jnp.float32, low / len(cuts), largest / len(cuts))
        level = level * jnp.repeat(jnp.exp(heights), shape[position] // parts).reshape((-1,) + (1,) * (len(shape) - 1 - position))
    return level


def bell_draw(own_key, dims, width, bound, pieces=(), held_as=jnp.bfloat16):
    entries = width * jax.random.normal(own_key, dims, jnp.float32)
    if pieces:
        entries = entries * steps_of(own_key, dims, pieces, -0.22, 0.18)
    return jnp.clip(entries, -bound, bound).astype(held_as)


def setup_inputs(seed: int = 0) -> dict:
    seeds = jax.random.split(jax.random.key(seed), 9)
    return {
        "tokens": bell_draw(seeds[0], (TOKENS, D), 1.0, 6.0, ((0, 32), (1, 8))),
        "cotangent": bell_draw(seeds[1], (TOKENS, D), 1.0, 6.0, ((0, 32), (1, 8))),
        "gate_blocks": bell_draw(seeds[2], (NPANEL, SLOTS, BLK, BLK), (3 * BLK) ** -0.5, 0.3125, ((0, 128),)),
        "up_blocks": bell_draw(seeds[3], (NPANEL, SLOTS, BLK, BLK), (3 * BLK) ** -0.5, 0.3125, ((0, 128),)),
        "down_blocks": bell_draw(seeds[4], (NPANEL, SLOTS, BLK, BLK), (3 * FF // (D // BLK)) ** -0.5, 0.15625, ((0, 128),)),
        "gate_index": draw_gate_index(jax.random.fold_in(seeds[8], 71), 0),
        "up_index": draw_up_index(jax.random.fold_in(seeds[8], 71), 0),
        "down_index": draw_down_index(jax.random.fold_in(seeds[8], 71), 0),
    }


def rounded(values):
    return lax.optimization_barrier(values.astype(jnp.bfloat16)).astype(jnp.float32)


def reference(tokens, cotangent, gate_blocks, up_blocks, down_blocks, gate_index, up_index, down_index):
    block_count = D // BLK
    row_count = tokens.shape[0]
    groups = row_count // TOK_GRP
    token_blocks = tokens.astype(jnp.float32).reshape(row_count, block_count, BLK)
    cotan_blocks = cotangent.astype(jnp.float32).reshape(row_count, block_count, BLK)
    per_group = FF // BLK // N_ROW

    def one_panel(totals, panel_item):
        out_acc, in_acc = totals
        w_gate, w_up, w_down, slot_gate, slot_up, slot_down = panel_item
        live_gate = (slot_gate < block_count).astype(jnp.float32)
        live_up = (slot_up < block_count).astype(jnp.float32)
        live_down = (slot_down < block_count).astype(jnp.float32)
        safe_gate = jnp.minimum(slot_gate, block_count - 1).astype(jnp.int32)
        safe_up = jnp.minimum(slot_up, block_count - 1).astype(jnp.int32)
        safe_down = jnp.minimum(slot_down, block_count - 1).astype(jnp.int32)
        w_gate = w_gate.astype(jnp.float32) * live_gate[:, None, None]
        w_up = w_up.astype(jnp.float32) * live_up[:, None, None]
        w_down = w_down.astype(jnp.float32) * live_down[:, None, None]
        x_gate = jnp.take(token_blocks, safe_gate, axis=1)
        x_up = jnp.take(token_blocks, safe_up, axis=1)
        dy_down = jnp.take(cotan_blocks, safe_down, axis=1)
        gate = jnp.einsum("tsb,sbo->to", x_gate, w_gate)
        up_value = jnp.einsum("tsb,sbo->to", x_up, w_up)
        sigmoid_gate = jax.nn.sigmoid(gate)
        swish_gate = gate * sigmoid_gate
        activated = rounded(swish_gate * up_value)
        out_acc = out_acc.at[:, safe_down].add(jnp.einsum("ti,sio->tso", activated, w_down))
        act_grad = jnp.einsum("tso,sio->ti", dy_down, w_down)
        silu_slope = sigmoid_gate * (1.0 + gate * (1.0 - sigmoid_gate))
        gate_delta = rounded(act_grad * up_value * silu_slope)
        up_delta = rounded(act_grad * swish_gate)
        in_acc = in_acc.at[:, safe_gate].add(jnp.einsum("to,sbo->tsb", gate_delta, w_gate))
        in_acc = in_acc.at[:, safe_up].add(jnp.einsum("to,sbo->tsb", up_delta, w_up))
        x_gate_g = x_gate.reshape(groups, TOK_GRP, SLOTS, BLK)
        x_up_g = x_up.reshape(groups, TOK_GRP, SLOTS, BLK)
        dy_down_g = dy_down.reshape(groups, TOK_GRP, SLOTS, BLK)
        gate_terms = jnp.einsum("gtsb,gto->gsbo", x_gate_g, gate_delta.reshape(groups, TOK_GRP, BLK))
        up_terms = jnp.einsum("gtsb,gto->gsbo", x_up_g, up_delta.reshape(groups, TOK_GRP, BLK))
        down_terms = jnp.einsum("gti,gtso->gsio", activated.reshape(groups, TOK_GRP, BLK), dy_down_g)
        gate_sum = jnp.sum(rounded(gate_terms), axis=0) * live_gate[:, None, None]
        up_sum = jnp.sum(rounded(up_terms), axis=0) * live_up[:, None, None]
        down_sum = jnp.sum(rounded(down_terms), axis=0) * live_down[:, None, None]
        return (out_acc, in_acc), (gate_sum, up_sum, down_sum)

    out_total = jnp.zeros((row_count, block_count, BLK), jnp.float32)
    in_total = jnp.zeros((row_count, block_count, BLK), jnp.float32)
    gate_parts, up_parts, down_parts = [], [], []
    for row_group in range(N_ROW):
        lower = row_group * per_group
        upper = lower + per_group
        zero_acc = jnp.zeros((row_count, block_count, BLK), jnp.float32)
        panel_items = (gate_blocks[lower:upper], up_blocks[lower:upper], down_blocks[lower:upper],
                       gate_index[lower:upper], up_index[lower:upper], down_index[lower:upper])
        (out_acc, in_acc), (gate_sum, up_sum, down_sum) = lax.scan(one_panel, (zero_acc, zero_acc), panel_items)
        out_total = out_total + rounded(out_acc)
        in_total = in_total + rounded(in_acc)
        gate_parts.append(gate_sum)
        up_parts.append(up_sum)
        down_parts.append(down_sum)
    block_output = out_total.reshape(row_count, D).astype(jnp.bfloat16)
    input_grad = in_total.reshape(row_count, D).astype(jnp.bfloat16)
    return (block_output, input_grad, jnp.concatenate(gate_parts, axis=0),
            jnp.concatenate(up_parts, axis=0), jnp.concatenate(down_parts, axis=0))
```

```python
import jax
import jax.numpy as jnp
from jax import lax
from jax.experimental import pallas as pl
from jax.experimental.pallas import tpu as pltpu
from jax.sharding import PartitionSpec as P

BLK = 128
SLOTS = 4
GROUP = 8
NBLK = 32
F32 = jnp.float32
BF16 = jnp.bfloat16
MESH = pl.DeviceIdType.MESH

T_GATE, T_UP, T_DOWN, T_PREV_OUT, T_LAST_OUT, T_PREV_IN, T_LAST_IN = 0, 32, 64, 96, 128, 160, 224


def dot(a, b, dims):
    return lax.dot_general(a, b, (dims, ((), ())), preferred_element_type=F32)


def block_of(ref, place):
    return ref[place // 8, (place // 2) % 4, place % 2]


class Copies:
    def __init__(self, send_sem, recv_sem, neighbours):
        self.send_sem, self.recv_sem, self.neighbours = send_sem, recv_sem, neighbours
        self.made = {}

    def send(self, name, src, dst, way):
        number = len(self.made)
        copy = pltpu.make_async_remote_copy(
            src_ref=src,
            dst_ref=dst,
            send_sem=self.send_sem.at[number],
            recv_sem=self.recv_sem.at[number],
            device_id=self.neighbours[way],
            device_id_type=MESH,
        )
        copy.start()
        self.made[name] = copy

    def recv(self, name):
        self.made[name].wait_recv()

    def finish(self):
        for copy in self.made.values():
            copy.wait_send()


def add_into(dst, srcs, dims, rows=64):
    total = 1
    for size in dims[:-2]:
        total *= size
    per = dims[-2] // rows

    def body(i, _):
        index = []
        rest = i // per
        for size in reversed(dims[:-2]):
            index.insert(0, rest % size)
            rest = rest // size
        index = tuple(index) + (pl.ds(pl.multiple_of((i % per) * rows, rows), rows),)
        value = dst[index].astype(F32)
        for src in srcs:
            value = value + src[index].astype(F32)
        dst[index] = value.astype(dst.dtype)
        return 0

    lax.fori_loop(0, total * per, body, 0)


def kernel(
    table, tokens, cotangent, gate_blocks, up_blocks, down_blocks,
    out_ref, in_ref, gate_grad, up_grad, down_grad,
    xt, xc, w, s_out, s_in, act_s, gd_s, ud_s, b_out, b_in, grads,
    ra, rb, qa, qb, g_sib, rz_half, rz,
    local_sem, send_sem, recv_sem,
):
    core = lax.axis_index("dp")
    row = lax.axis_index("row")
    col = lax.axis_index("col")
    y, xh, xl, z = row // 2, row % 2, col // 8, col % 8
    x = xh * 2 + xl

    def at(core=core, x=x, y=y, z=z):
        return (core, y * 2 + x // 2, (x % 2) * 8 + z)

    xs = [(x + o) % 4 for o in range(4)]
    ys = [(y + o) % 4 for o in range(4)]
    zs = [(z + o) % 8 for o in range(8)]
    ways = {
        "x+": at(x=xs[1]), "x-": at(x=xs[3]), "y+": at(y=ys[1]), "y-": at(y=ys[3]),
        "z+": at(z=zs[1]), "z-": at(z=zs[7]), "c": at(core=1 - core),
    }
    cp = Copies(send_sem, recv_sem, ways)

    barrier = pltpu.get_barrier_semaphore()
    for way in ways.values():
        pl.semaphore_signal(barrier, inc=1, device_id=way, device_id_type=MESH)

    def half(x_):
        return pl.ds(pl.multiple_of((x_ % 2) * 128, 128), 128)

    local = []

    def copy_in(src, dst):
        copy = pltpu.make_async_copy(src, dst, local_sem.at[len(local)])
        copy.start()
        local.append(copy)

    for src, dst in ((tokens, xt), (cotangent, xc)):
        for hj in range(4):
            copy_in(src.at[:, pl.ds(hj * BLK, BLK)], dst.at[hj, y, xh, half(x)])
    for i, src in enumerate((gate_blocks, up_blocks, down_blocks)):
        copy_in(src.at[0], w.at[i, z])
    zero = jnp.zeros((256, BLK), BF16)
    xt[4, 0, 0] = zero
    xc[4, 0, 0] = zero
    s_out[NBLK] = jnp.zeros((256, BLK), F32)
    s_in[2 * NBLK] = jnp.zeros((256, BLK), F32)
    for copy in local:
        copy.wait()
    pl.semaphore_wait(barrier, len(ways))

    def piece(ref, hj, n, y_, x_):
        return ref.at[pl.ds(hj, n), y_, x_ // 2, half(x_)]

    def line_x(ref, hj, y_):
        return ref.at[hj, y_]

    def line_y(ref, hj, x_):
        return ref.at[hj, :, x_ // 2, half(x_)]

    def send_same(name, ref, way):
        cp.send(name, ref, ref, way)

    def gather_a(t, ref):
        for way in ("x+", "x-"):
            send_same((t, "a", way), piece(ref, 0, 2, y, x), way)
        for way in ("y+", "y-"):
            send_same((t, "a", way), piece(ref, 2, 2, y, x), way)

    def gather_b(t, ref):
        cp.recv((t, "a", "x+"))
        send_same((t, "b", "x+"), piece(ref, 0, 1, y, xs[3]), "x+")
        cp.recv((t, "a", "x-"))
        send_same((t, "b", "x-"), piece(ref, 1, 1, y, xs[1]), "x-")
        cp.recv((t, "a", "y+"))
        send_same((t, "b", "y+"), piece(ref, 2, 1, ys[3], x), "y+")
        cp.recv((t, "a", "y-"))
        send_same((t, "b", "y-"), piece(ref, 3, 1, ys[1], x), "y-")

    def gather_c(t, ref):
        cp.recv((t, "b", "x+"))
        cp.recv((t, "b", "x-"))
        for hj, way in ((0, "y+"), (1, "y-"), (1, "y+"), (0, "y-")):
            send_same((t, "c", way, hj), line_x(ref, hj, y), way)
        cp.recv((t, "b", "y+"))
        cp.recv((t, "b", "y-"))
        for hj, way in ((2, "x+"), (3, "x-"), (3, "x+"), (2, "x-")):
            send_same((t, "c", way, hj), line_y(ref, hj, x), way)

    def gather_d(t, ref):
        cp.recv((t, "c", "y+", 0))
        send_same((t, "d", "y+"), line_x(ref, 0, ys[3]), "y+")
        cp.recv((t, "c", "y-", 1))
        send_same((t, "d", "y-"), line_x(ref, 1, ys[1]), "y-")
        cp.recv((t, "c", "x+", 2))
        send_same((t, "d", "x+"), line_y(ref, 2, xs[3]), "x+")
        cp.recv((t, "c", "x-", 3))
        send_same((t, "d", "x-"), line_y(ref, 3, xs[1]), "x-")

    def gather_end(t):
        for hj, way in ((1, "y+"), (0, "y-"), (3, "x+"), (2, "x-")):
            cp.recv((t, "c", way, hj))
        for way in ("y+", "y-", "x+", "x-"):
            cp.recv((t, "d", way))

    mine = core * 2

    def w_piece(o, first=0, n=2):
        return w.at[:, zs[o % 8], pl.ds(mine + first, n)]

    def weights_first():
        send_same(("w", 1, "z+"), w_piece(0), "z+")
        send_same(("w", 1, "z-"), w_piece(0), "z-")

    def weights_step(k):
        cp.recv(("w", k, "z+"))
        if k < 3:
            send_same(("w", k + 1, "z+"), w_piece(-k), "z+")
        if k == 3:
            send_same(("w", 4, "z+"), w_piece(-3, 0, 1), "z+")
        cp.recv(("w", k, "z-"))
        if k < 3:
            send_same(("w", k + 1, "z-"), w_piece(k), "z-")
        if k == 3:
            send_same(("w", 4, "z-"), w_piece(3, 1, 1), "z-")
        send_same(("ws", k), w_piece(-k), "c")
        if k < 4:
            send_same(("ws", -k), w_piece(k), "c")

    def weights_end():
        for k in (1, 2, 3, 4, -1, -2, -3):
            cp.recv(("ws", k))

    gather_a("t", xt)
    gather_a("c", xc)
    weights_first()
    gather_b("t", xt)
    gather_b("c", xc)
    gather_c("t", xt)
    weights_step(1)
    gather_c("c", xc)
    gather_d("t", xt)
    weights_step(2)
    weights_step(3)
    gather_end("t")
    gather_d("c", xc)
    weights_step(4)
    weights_end()
    gather_end("c")

    def picked(ref, first, p):
        return jnp.concatenate(
            [block_of(ref, table[first + p * SLOTS + s]) for s in range(SLOTS)], axis=1
        )

    def w_rows(i, p):
        return w[i, p].reshape(SLOTS * BLK, BLK)

    def w_lanes(i, p):
        return jnp.concatenate([w[i, p, s] for s in range(SLOTS)], axis=1)

    def forward(p, _):
        gate = dot(picked(xt, T_GATE, p), w_rows(0, p), ((1,), (0,)))
        up = dot(picked(xt, T_UP, p), w_rows(1, p), ((1,), (0,)))
        sig = jax.nn.sigmoid(gate)
        swish = gate * sig
        act = (swish * up).astype(BF16)
        act_s[p] = act
        wd = w_lanes(2, p)
        spread = dot(act, wd, ((1,), (0,)))
        for s in range(SLOTS):
            e = p * SLOTS + s
            s_out[e] = s_out[table[T_PREV_OUT + e]] + spread[:, s * BLK:(s + 1) * BLK]
        act_grad = dot(picked(xc, T_DOWN, p), wd, ((1,), (1,)))
        slope = sig * (1.0 + gate * (1.0 - sig))
        gd_s[p] = (act_grad * up * slope).astype(BF16)
        ud_s[p] = (act_grad * swish).astype(BF16)
        return 0

    lax.fori_loop(0, GROUP, forward, 0)

    def collect(dst, src, first):
        def body(q, _):
            dst[q // 8, (q // 2) % 4, q % 2] = src[table[first + q]].astype(BF16)
            return 0

        lax.fori_loop(0, NBLK, body, 0)

    def stage(t, name, axis, hj, part, bufs, dims):
        near = xs if axis == "x" else ys
        plus, minus = axis + "+", axis + "-"
        b1, b2, b3 = bufs

        def first():
            cp.send((t, name, 1, plus), part(hj, near[2]), b1.at[0], plus)
            cp.send((t, name, 1, minus), part(hj + 1, near[2]), b1.at[1], minus)
            cp.send((t, name, 2, plus), part(hj + 1, near[1]), b2.at[0], plus)
            cp.send((t, name, 2, minus), part(hj, near[3]), b2.at[1], minus)

        def second():
            cp.recv((t, name, 1, plus))
            add_into(part(hj, near[1]), [b1.at[0]], dims)
            cp.send((t, name, 3, plus), part(hj, near[1]), b3.at[0], plus)
            cp.recv((t, name, 1, minus))
            add_into(part(hj + 1, near[3]), [b1.at[1]], dims)
            cp.send((t, name, 3, minus), part(hj + 1, near[3]), b3.at[1], minus)

        def third():
            cp.recv((t, name, 2, plus))
            cp.recv((t, name, 2, minus))
            cp.recv((t, name, 3, plus))
            add_into(part(hj, near[0]), [b3.at[0], b2.at[1]], dims)
            cp.recv((t, name, 3, minus))
            add_into(part(hj + 1, near[0]), [b2.at[0], b3.at[1]], dims)

        return first, second, third

    def reduce_of(k, t, ref):
        def along_x(hj, y_):
            return ref.at[hj, y_]

        def along_y(hj, x_):
            return ref.at[hj, :, x_ // 2, half(x_)]

        def end_x(hj, x_):
            return ref.at[hj, y, x_ // 2, half(x_)]

        def end_y(hj, y_):
            return ref.at[hj, y_, xh, half(x)]

        y1 = stage(t, "y1", "y", 0, along_x, [ra.at[k, i] for i in range(3)], (2, 256, BLK))
        x1 = stage(t, "x1", "x", 2, along_y, [rb.at[k, i] for i in range(3)], (4, 128, BLK))
        x2 = stage(t, "x2", "x", 0, end_x, [qa.at[k, i] for i in range(3)], (128, BLK))
        y2 = stage(t, "y2", "y", 2, end_y, [qb.at[k, i] for i in range(3)], (128, BLK))
        return y1, x1, x2, y2

    o_y1, o_x1, o_x2, o_y2 = reduce_of(0, "o", b_out)
    i_y1, i_x1, i_x2, i_y2 = reduce_of(1, "i", b_in)

    collect(b_out, s_out, T_LAST_OUT)
    o_y1[0]()
    o_x1[0]()

    def backward(p, _):
        for i, delta in ((0, gd_s), (1, ud_s)):
            back = dot(delta[p], w_rows(i, p), ((1,), (1,)))
            for s in range(SLOTS):
                e = p * 8 + i * SLOTS + s
                s_in[e] = s_in[table[T_PREV_IN + e]] + back[:, s * BLK:(s + 1) * BLK]
        return 0

    lax.fori_loop(0, GROUP, backward, 0)
    collect(b_in, s_in, T_LAST_IN)
    o_y1[1]()
    o_x1[1]()
    i_y1[0]()
    i_x1[0]()

    def down_term(p, _):
        term = dot(act_s[p], picked(xc, T_DOWN, p), ((0,), (0,)))
        for s in range(SLOTS):
            grads[2, p, s] = term[:, s * BLK:(s + 1) * BLK].astype(BF16)
        return 0

    def in_term(i, first, delta):
        def body(p, _):
            term = dot(picked(xt, first, p), delta[p], ((0,), (0,)))
            grads[i, p] = term.astype(BF16).reshape(SLOTS, BLK, BLK)
            return 0

        return body

    theirs = (1 - core) * 2

    def sibling(i):
        cp.send(("gs", i), grads.at[i, :, pl.ds(theirs, 2)], g_sib.at[i], "c")

    lax.fori_loop(0, GROUP, down_term, 0)
    sibling(2)
    lax.fori_loop(0, GROUP, in_term(0, T_GATE, gd_s), 0)
    sibling(0)
    lax.fori_loop(0, GROUP, in_term(1, T_UP, ud_s), 0)
    sibling(1)

    def g_part(i, o, first=0, n=2):
        return grads.at[i, zs[o % 8], pl.ds(mine + first, n)]

    def z_first(i):
        cp.recv(("gs", i))
        add_into(grads.at[i, :, pl.ds(mine, 2)], [g_sib.at[i]], (8, 2, 128, BLK))
        cp.send(("z", i, 1, "z+"), g_part(i, 4, 0, 1), rz_half.at[i, pl.ds(0, 1)], "z+")
        cp.send(("z", i, 1, "z-"), g_part(i, 4, 1, 1), rz_half.at[i, pl.ds(1, 1)], "z-")

    def z_step(i, k):
        cp.recv(("z", i, k, "z+"))
        o = 4 - k
        if k == 1:
            add_into(g_part(i, o, 0, 1), [rz_half.at[i, pl.ds(0, 1)]], (1, 128, BLK))
        else:
            add_into(g_part(i, o), [rz.at[i, k - 2, 0]], (2, 128, BLK))
        cp.send(("z", i, k + 1, "z+"), g_part(i, o), rz.at[i, k - 1, 0], "z+")
        cp.recv(("z", i, k, "z-"))
        if k == 1:
            add_into(g_part(i, -o, 1, 1), [rz_half.at[i, pl.ds(1, 1)]], (1, 128, BLK))
        else:
            add_into(g_part(i, -o), [rz.at[i, k - 2, 1]], (2, 128, BLK))
        cp.send(("z", i, k + 1, "z-"), g_part(i, -o), rz.at[i, k - 1, 1], "z-")

    grad_refs = (gate_grad, up_grad, down_grad)

    def z_last(i):
        cp.recv(("z", i, 4, "z+"))
        cp.recv(("z", i, 4, "z-"))
        ref = grad_refs[i]

        def body(n, _):
            rows = pl.ds(pl.multiple_of((n % 2) * 64, 64), 64)
            s = n // 2
            ref[0, mine + s, rows] = (
                grads[i, z, mine + s, rows].astype(F32)
                + rz[i, 2, 0, s, rows].astype(F32)
                + rz[i, 2, 1, s, rows].astype(F32)
            )
            return 0

        lax.fori_loop(0, 4, body, 0)
        part = ref.at[0, pl.ds(mine, 2)]
        cp.send(("gf", i), part, part, "c")

    order = (2, 0, 1)
    z_first(2)
    z_first(0)
    z_first(1)
    o_y1[2]()
    o_x2[0]()
    o_x1[2]()
    o_y2[0]()
    for i in order:
        z_step(i, 1)
    o_x2[1]()
    o_y2[1]()
    i_y1[1]()
    i_x1[1]()
    for i in order:
        z_step(i, 2)
    o_x2[2]()
    o_y2[2]()
    i_y1[2]()
    i_x2[0]()
    i_x1[2]()
    i_y2[0]()
    for i in order:
        z_step(i, 3)
    i_x2[1]()
    i_y2[1]()
    for i in order:
        z_last(i)
    i_x2[2]()
    i_y2[2]()

    for hj in range(4):
        out_ref[:, hj * BLK:(hj + 1) * BLK] = b_out[hj, y, xh, half(x)]
        in_ref[:, hj * BLK:(hj + 1) * BLK] = b_in[hj, y, xh, half(x)]
    for i in order:
        cp.recv(("gf", i))
    cp.finish()


def chain(keys, count):
    number = jnp.arange(count, dtype=jnp.int32)
    same = (keys[:, None] == keys[None, :]) & (number[None, :] < number[:, None])
    prev = jnp.max(jnp.where(same, number[None, :], -1), axis=1)
    places = jnp.arange(NBLK, dtype=jnp.int32)
    last = jnp.max(jnp.where(keys[None, :] == places[:, None], number[None, :], -1), axis=1)
    return jnp.where(prev < 0, count, prev), jnp.where(last < 0, count, last)


def per_device(
    tokens, cotangent, gate_blocks, up_blocks, down_blocks, gate_index, up_index, down_index
):
    line = (lax.axis_index("row") * 2 + lax.axis_index("col") // GROUP) * GROUP

    def places(index):
        mine = lax.dynamic_slice_in_dim(index, line, GROUP, 0)
        return jnp.where(mine < NBLK, (mine % 4) * 8 + mine // 4, NBLK).astype(jnp.int32)

    gate, up, down = places(gate_index), places(up_index), places(down_index)
    prev_out, last_out = chain(down.reshape(-1), NBLK)
    prev_in, last_in = chain(jnp.concatenate((gate, up), axis=1).reshape(-1), 2 * NBLK)
    table = jnp.concatenate(
        (gate.reshape(-1), up.reshape(-1), down.reshape(-1), prev_out, last_out, prev_in, last_in)
    )
    any_spec = pl.BlockSpec(memory_space=pl.ANY)
    vmem_spec = pl.BlockSpec(memory_space=pltpu.VMEM)
    grad = jax.ShapeDtypeStruct((1, SLOTS, BLK, BLK), F32)
    act = jax.ShapeDtypeStruct((128, 4 * BLK), BF16)
    big = (4, 4, 2, 256, BLK)
    count = 140
    return pl.pallas_call(
        kernel,
        out_shape=(act, act, grad, grad, grad),
        in_specs=[pl.BlockSpec(memory_space=pltpu.SMEM)] + [any_spec] * 5,
        out_specs=(vmem_spec,) * 5,
        scratch_shapes=[
            pltpu.VMEM((5, 4, 2, 256, BLK), BF16),
            pltpu.VMEM((5, 4, 2, 256, BLK), BF16),
            pltpu.VMEM((3, GROUP, SLOTS, BLK, BLK), BF16),
            pltpu.VMEM((NBLK + 1, 256, BLK), F32),
            pltpu.VMEM((2 * NBLK + 1, 256, BLK), F32),
            pltpu.VMEM((GROUP, 256, BLK), BF16),
            pltpu.VMEM((GROUP, 256, BLK), BF16),
            pltpu.VMEM((GROUP, 256, BLK), BF16),
            pltpu.VMEM(big, BF16),
            pltpu.VMEM(big, BF16),
            pltpu.VMEM((3, GROUP, SLOTS, BLK, BLK), BF16),
            pltpu.VMEM((2, 3, 2, 2, 256, BLK), BF16),
            pltpu.VMEM((2, 3, 2, 4, 128, BLK), BF16),
            pltpu.VMEM((2, 3, 2, 128, BLK), BF16),
            pltpu.VMEM((2, 3, 2, 128, BLK), BF16),
            pltpu.VMEM((3, GROUP, 2, BLK, BLK), BF16),
            pltpu.VMEM((3, 2, BLK, BLK), BF16),
            pltpu.VMEM((3, 3, 2, 2, BLK, BLK), BF16),
            pltpu.SemaphoreType.DMA((11,)),
            pltpu.SemaphoreType.DMA((count,)),
            pltpu.SemaphoreType.DMA((count,)),
        ],
        compiler_params=pltpu.CompilerParams(
            collective_id=0, has_side_effects=True, vmem_limit_bytes=56 << 20
        ),
        name="ffn",
    )(table, tokens, cotangent, gate_blocks, up_blocks, down_blocks)


def solution(mesh):
    act = P(("dp", "col"), "row")
    blocks = P(("row", "col"), None, None, None)
    return jax.shard_map(
        per_device,
        mesh=mesh,
        in_specs=(act, act, blocks, blocks, blocks, P(), P(), P()),
        out_specs=(act, act, blocks, blocks, blocks),
        check_vma=False,
    )
```

```python
import jax
import jax.numpy as jnp
from jax import lax
from jax.experimental import pallas as pl
from jax.experimental.pallas import tpu as pltpu
from jax.sharding import PartitionSpec as P

BLK = 128
SLOTS = 4
GROUP = 8
NBLK = 32
F32 = jnp.float32
BF16 = jnp.bfloat16
MESH = pl.DeviceIdType.MESH

T_GATE, T_UP, T_DOWN, T_PREV_OUT, T_PREV_GATE, T_PREV_UP, T_LAST_OUT, T_LAST_IN = 0, 4, 8, 12, 16, 20, 24, 56
T_ROWS = 88
I32 = jnp.int32


def dot(a, b, dims):
    return lax.dot_general(a, b, (dims, ((), ())), preferred_element_type=F32)


def block_of(ref, place):
    return ref[place // 8, (place // 2) % 4, place % 2]


class Copies:
    def __init__(self, send_sem, recv_sem, neighbours):
        self.send_sem, self.recv_sem, self.neighbours = send_sem, recv_sem, neighbours
        self.made = {}

    def send(self, name, src, dst, way):
        number = len(self.made)
        copy = pltpu.make_async_remote_copy(
            src_ref=src,
            dst_ref=dst,
            send_sem=self.send_sem.at[number],
            recv_sem=self.recv_sem.at[number],
            device_id=self.neighbours[way],
            device_id_type=MESH,
        )
        copy.start()
        self.made[name] = copy

    def recv(self, name):
        self.made[name].wait_recv()

    def finish(self):
        for copy in self.made.values():
            copy.wait_send()


def add_into(dst, srcs, dims, rows=64):
    total = 1
    for size in dims[:-2]:
        total *= size
    per = dims[-2] // rows

    def body(i, _):
        index = []
        rest = i // per
        for size in reversed(dims[:-2]):
            index.insert(0, rest % size)
            rest = rest // size
        index = tuple(index) + (pl.ds(pl.multiple_of((i % per) * rows, rows), rows),)
        value = dst[index].astype(F32)
        for src in srcs:
            value = value + src[index].astype(F32)
        dst[index] = value.astype(dst.dtype)
        return 0

    lax.fori_loop(0, total * per, body, 0)


def make_table(keys, tab, first):
    lane = lax.broadcasted_iota(I32, (SLOTS, BLK), 1)
    panel = lane & 7

    def place(v):
        return jnp.where(v < NBLK, (v & 3) * 8 + (v >> 2), NBLK)

    gate, up, down = (place(keys[i]) for i in range(3))
    tab[T_GATE:T_GATE + SLOTS] = gate
    tab[T_UP:T_UP + SLOTS] = up
    tab[T_DOWN:T_DOWN + SLOTS] = down

    prev_out = jnp.full((SLOTS, BLK), NBLK, I32)
    prev_gate = jnp.full((SLOTS, BLK), 2 * NBLK, I32)
    prev_up = prev_gate
    for d in range(GROUP - 1, -1, -1):
        far = panel >= d
        if d:
            moved = pltpu.roll(down, d, axis=1)
            for s in range(SLOTS):
                hit = (down == moved[s:s + 1]) & far
                prev_out = jnp.where(hit, (panel - d) * SLOTS + s, prev_out)
        for i, src in enumerate((gate, up)):
            if d == 0 and i == 1:
                continue
            moved = pltpu.roll(src, d, axis=1) if d else src
            for s in range(SLOTS):
                number = (panel - d) * 8 + i * SLOTS + s
                if d:
                    prev_gate = jnp.where((gate == moved[s:s + 1]) & far, number, prev_gate)
                prev_up = jnp.where((up == moved[s:s + 1]) & far, number, prev_up)
    tab[T_PREV_OUT:T_PREV_OUT + SLOTS] = prev_out
    tab[T_PREV_GATE:T_PREV_GATE + SLOTS] = prev_gate
    tab[T_PREV_UP:T_PREV_UP + SLOTS] = prev_up

    wanted = lax.broadcasted_iota(I32, (NBLK, BLK), 0)
    ours = lax.broadcasted_iota(I32, (NBLK, BLK), 1) - first
    inside = (ours >= 0) & (ours < GROUP)

    def last(sources, per):
        best = jnp.full((NBLK, BLK), -1, I32)
        for i, src in enumerate(sources):
            for s in range(SLOTS):
                hit = (wanted == src[s:s + 1]) & inside
                best = jnp.maximum(best, jnp.where(hit, ours * per + i * SLOTS + s, -1))
        best = jnp.max(best, axis=1, keepdims=True)
        best = jnp.where(best < 0, per * GROUP, best)
        return jnp.broadcast_to(best, (NBLK, BLK))

    tab[T_LAST_OUT:T_LAST_OUT + NBLK] = last((down,), SLOTS)
    tab[T_LAST_IN:T_LAST_IN + NBLK] = last((gate, up), 2 * SLOTS)


def kernel(
    gate_index, up_index, down_index, tokens, cotangent, gate_blocks, up_blocks, down_blocks,
    out_ref, in_ref, grad_ref,
    keys, tab, table, xt, xc, turned, w, s_out, s_in, act_s, gd_s, ud_s, swish_s, slope_s,
    b_out, b_in, grads, ra, rb, qa, qb, g_sib, rz,
    key_sem, local_sem, send_sem, recv_sem,
):
    core = lax.axis_index("dp")
    row = lax.axis_index("row")
    col = lax.axis_index("col")
    y, xh, xl, z = row // 2, row % 2, col // 8, col % 8
    x = xh * 2 + xl

    def at(core=core, x=x, y=y, z=z):
        return (core, y * 2 + x // 2, (x % 2) * 8 + z)

    xs = [(x + o) % 4 for o in range(4)]
    ys = [(y + o) % 4 for o in range(4)]
    zs = [(z + o) % 8 for o in range(8)]
    ways = {
        "x+": at(x=xs[1]), "x-": at(x=xs[3]), "y+": at(y=ys[1]), "y-": at(y=ys[3]),
        "z+": at(z=zs[1]), "z-": at(z=zs[7]), "c": at(core=1 - core),
    }
    cp = Copies(send_sem, recv_sem, ways)

    barrier = pltpu.get_barrier_semaphore()
    for way in ways.values():
        pl.semaphore_signal(barrier, inc=1, device_id=way, device_id_type=MESH)

    def half(x_):
        return pl.ds(pl.multiple_of((x_ % 2) * 128, 128), 128)

    local = {}

    def copy_in(name, src, dst):
        copy = pltpu.make_async_copy(src, dst, local_sem.at[len(local)])
        copy.start()
        local[name] = copy

    for t, src, dst in (("t", tokens, xt), ("c", cotangent, xc)):
        for hj in range(4):
            copy_in((t, hj), src.at[:, pl.ds(hj * BLK, BLK)], dst.at[hj, y, xh, half(x)])
    for i, src in enumerate((gate_blocks, up_blocks, down_blocks)):
        copy_in(("w", i), src.at[0], w.at[i, z])
    for i, src in enumerate((gate_index, up_index, down_index)):
        copy_in(("k", i), src, keys.at[i])
    pl.semaphore_wait(barrier, len(ways))

    def landed(name, count):
        for i in range(count):
            local[name, i].wait()

    def piece(ref, hj, n, y_, x_):
        return ref.at[pl.ds(hj, n), y_, x_ // 2, half(x_)]

    def line_x(ref, hj, y_):
        return ref.at[hj, y_]

    def line_y(ref, hj, x_):
        return ref.at[hj, :, x_ // 2, half(x_)]

    def send_same(name, ref, way):
        cp.send(name, ref, ref, way)

    def gather_a(t, ref):
        for way in ("x+", "x-"):
            send_same((t, "a", way), piece(ref, 0, 2, y, x), way)
        for way in ("y+", "y-"):
            send_same((t, "a", way), piece(ref, 2, 2, y, x), way)

    def gather_b(t, ref, way):
        cp.recv((t, "a", way))
        hj, y_, x_ = {
            "x+": (0, y, xs[3]), "x-": (1, y, xs[1]), "y+": (2, ys[3], x), "y-": (3, ys[1], x),
        }[way]
        send_same((t, "b", way), piece(ref, hj, 1, y_, x_), way)

    def gather_c1(t, ref):
        cp.recv((t, "b", "x+"))
        cp.recv((t, "b", "x-"))
        for hj, way in ((0, "y+"), (1, "y-"), (1, "y+"), (0, "y-")):
            send_same((t, "c", way, hj), line_x(ref, hj, y), way)

    def gather_c2(t, ref):
        cp.recv((t, "b", "y+"))
        cp.recv((t, "b", "y-"))
        for hj, way in ((2, "x+"), (3, "x-"), (3, "x+"), (2, "x-")):
            send_same((t, "c", way, hj), line_y(ref, hj, x), way)

    def gather_d(t, ref, way):
        hj = {"y+": 0, "y-": 1, "x+": 2, "x-": 3}[way]
        cp.recv((t, "c", way, hj))
        part = {
            "y+": line_x(ref, 0, ys[3]), "y-": line_x(ref, 1, ys[1]),
            "x+": line_y(ref, 2, xs[3]), "x-": line_y(ref, 3, xs[1]),
        }[way]
        send_same((t, "d", way), part, way)

    def gather_end(t):
        for hj, way in ((1, "y+"), (0, "y-"), (3, "x+"), (2, "x-")):
            cp.recv((t, "c", way, hj))
        for way in ("y+", "y-", "x+", "x-"):
            cp.recv((t, "d", way))

    mine = core * 2

    def w_piece(i, o, first=0, n=2):
        return w.at[i, zs[o % 8], pl.ds(mine + first, n)]

    def weights_first(i):
        for way in ("z+", "z-"):
            send_same(("w", i, 1, way), w_piece(i, 0), way)

    def weights_step(i, k, way):
        o, first = (-k, 0) if way == "z+" else (k, 1)
        cp.recv(("w", i, k, way))
        if k < 3:
            send_same(("w", i, k + 1, way), w_piece(i, o), way)
        else:
            send_same(("w", i, 4, way), w_piece(i, o, first, 1), way)
        send_same(("ws", i, -o), w_piece(i, o), "c")

    def weights_far(i):
        cp.recv(("w", i, 4, "z+"))
        cp.recv(("w", i, 4, "z-"))
        send_same(("ws", i, 4), w_piece(i, 4), "c")

    def weights_end(i):
        for k in (1, 2, 3, 4, -1, -2, -3):
            cp.recv(("ws", i, k))

    line = (row * 2 + xl) * GROUP
    def picked(ref, first, p, axis=1):
        return jnp.concatenate(
            [block_of(ref, table[first + s, line + p]) for s in range(SLOTS)], axis=axis
        )

    def w_rows(i, p):
        return w[i, p].reshape(SLOTS * BLK, BLK)

    def w_lanes(i, p):
        return jnp.concatenate([w[i, p, s] for s in range(SLOTS)], axis=1)

    def forward(p, _):
        gate = dot(picked(xt, T_GATE, p), w_rows(0, p), ((1,), (0,)))
        up = dot(picked(xt, T_UP, p), w_rows(1, p), ((1,), (0,)))
        sig = jax.nn.sigmoid(gate)
        swish = gate * sig
        act = (swish * up).astype(BF16)
        act_s[p] = act
        swish_s[p] = swish
        slope_s[p] = up * (sig * (1.0 + gate * (1.0 - sig)))
        return 0

    def spread_out(p, _):
        spread = dot(act_s[p], w_lanes(2, p), ((1,), (0,)))
        for s in range(SLOTS):
            before = table[T_PREV_OUT + s, line + p]
            s_out[p * SLOTS + s] = s_out[before] + spread[:, s * BLK:(s + 1) * BLK]
        return 0

    def deltas(p, _):
        act_grad = dot(picked(xc, T_DOWN, p), w_lanes(2, p), ((1,), (1,)))
        gd_s[p] = (act_grad * slope_s[p]).astype(BF16)
        ud_s[p] = (act_grad * swish_s[p]).astype(BF16)
        return 0

    def backward(p, _):
        for i, delta, first in ((0, gd_s, T_PREV_GATE), (1, ud_s, T_PREV_UP)):
            back = dot(delta[p], w_rows(i, p), ((1,), (1,)))
            for s in range(SLOTS):
                before = table[first + s, line + p]
                s_in[p * 8 + i * SLOTS + s] = s_in[before] + back[:, s * BLK:(s + 1) * BLK]
        return 0

    def terms(j, _):
        odd = j % 2
        p = (z + 4 + (j // 2) * (1 - odd) - ((j + 1) // 2) * odd) % GROUP
        term = dot(act_s[p], picked(xc, T_DOWN, p), ((0,), (0,)))
        for s in range(SLOTS):
            grads[2, p, s] = term[:, s * BLK:(s + 1) * BLK].astype(BF16)
        for i, first, delta in ((0, T_GATE, gd_s), (1, T_UP, ud_s)):
            term = dot(picked(turned, first, p, axis=0), delta[p], ((1,), (0,)))
            grads[i, p] = term.astype(BF16).reshape(SLOTS, BLK, BLK)
        return 0

    def turn(q, _):
        turned[q // 8, (q // 2) % 4, q % 2] = xt[q // 8, (q // 2) % 4, q % 2].T
        return 0

    def panels(body, lower=0, upper=GROUP):
        lax.fori_loop(lower, upper, body, 0)

    def collect(dst, src, first):
        def body(q, _):
            dst[q // 8, (q // 2) % 4, q % 2] = src[table[first + q, 0]].astype(BF16)
            return 0

        lax.fori_loop(0, NBLK, body, 0)

    def stage(t, name, axis, hj, part, bufs, dims):
        near = xs if axis == "x" else ys
        plus, minus = axis + "+", axis + "-"
        b1, b2, b3 = bufs

        def first():
            cp.send((t, name, 1, plus), part(hj, near[2]), b1.at[0], plus)
            cp.send((t, name, 1, minus), part(hj + 1, near[2]), b1.at[1], minus)
            cp.send((t, name, 2, plus), part(hj + 1, near[1]), b2.at[0], plus)
            cp.send((t, name, 2, minus), part(hj, near[3]), b2.at[1], minus)

        def second(sign):
            way, part_, i = (
                (plus, part(hj, near[1]), 0) if sign == "+" else (minus, part(hj + 1, near[3]), 1)
            )
            cp.recv((t, name, 1, way))
            add_into(part_, [b1.at[i]], dims)
            cp.send((t, name, 3, way), part_, b3.at[i], way)

        def third():
            cp.recv((t, name, 2, plus))
            cp.recv((t, name, 2, minus))
            cp.recv((t, name, 3, plus))
            add_into(part(hj, near[0]), [b3.at[0], b2.at[1]], dims)
            cp.recv((t, name, 3, minus))
            add_into(part(hj + 1, near[0]), [b2.at[0], b3.at[1]], dims)

        return first, second, third

    def reduce_of(k, t, ref):
        def along_x(hj, y_):
            return ref.at[hj, y_]

        def along_y(hj, x_):
            return ref.at[hj, :, x_ // 2, half(x_)]

        def end_x(hj, x_):
            return ref.at[hj, y, x_ // 2, half(x_)]

        def end_y(hj, y_):
            return ref.at[hj, y_, xh, half(x)]

        y1 = stage(t, "y1", "y", 0, along_x, [ra.at[k, i] for i in range(3)], (2, 256, BLK))
        x1 = stage(t, "x1", "x", 2, along_y, [rb.at[k, i] for i in range(3)], (4, 128, BLK))
        x2 = stage(t, "x2", "x", 0, end_x, [qa.at[k, i] for i in range(3)], (128, BLK))
        y2 = stage(t, "y2", "y", 2, end_y, [qb.at[k, i] for i in range(3)], (128, BLK))
        return y1, x1, x2, y2

    o_y1, o_x1, o_x2, o_y2 = reduce_of(0, "o", b_out)
    i_y1, i_x1, i_x2, i_y2 = reduce_of(1, "i", b_in)

    theirs = (1 - core) * 2

    def sibling(o):
        p = zs[o % 8]
        cp.send(("gs", o), grads.at[:, p, pl.ds(theirs, 2)], g_sib.at[:, p], "c")

    def pair_sum(o):
        cp.recv(("gs", o))
        p = zs[o % 8]
        add_into(grads.at[:, p, pl.ds(mine, 2)], [g_sib.at[:, p]], (3, 2, 128, BLK))

    def z_send(way, k, s):
        d, sign, begins = (0, 1, 0) if way == "z+" else (1, -1, 1)
        part = grads.at[:, zs[sign * (5 - k) % 8], mine + s]
        if k > 2 or (k == 2 and s == begins):
            cp.recv(("z", way, k - 1, s))
            add_into(part, [rz.at[d, k - 2, s]], (3, 128, BLK))
        cp.send(("z", way, k, s), part, rz.at[d, k - 1, s], way)

    def z_last(s):
        cp.recv(("z", "z+", 4, s))
        cp.recv(("z", "z-", 4, s))

        def body(n, _):
            rows = pl.ds(pl.multiple_of((n % 2) * 64, 64), 64)
            i = n // 2
            grad_ref[i, mine + s, rows] = (
                grads[i, z, mine + s, rows].astype(F32)
                + rz[0, 3, s, i, rows].astype(F32)
                + rz[1, 3, s, i, rows].astype(F32)
            )
            return 0

        lax.fori_loop(0, 6, body, 0)
        part = grad_ref.at[:, mine + s]
        cp.send(("gf", s), part, part, "c")

    table_copy = pltpu.make_async_copy(tab, table, key_sem.at[0])

    def table_start():
        landed("k", 3)
        make_table(keys, tab, line)
        table_copy.start()

    def zeros():
        for ref in (xt, xc):
            ref[4, 0, 0] = jnp.zeros((256, BLK), BF16)
        turned[4, 0, 0] = jnp.zeros((BLK, 256), BF16)
        s_out[NBLK] = jnp.zeros((256, BLK), F32)
        s_in[2 * NBLK] = jnp.zeros((256, BLK), F32)

    def turn_some(lower, upper):
        lax.fori_loop(lower, upper, turn, 0)

    def write_out(ref, b):
        for hj in range(4):
            ref[:, hj * BLK:(hj + 1) * BLK] = b[hj, y, xh, half(x)]

    landed("t", 4)
    gather_a("t", xt)
    landed("w", 3)
    landed("c", 4)
    weights_first(0)
    weights_first(1)
    gather_a("c", xc)
    weights_first(2)
    table_start()
    table_copy.wait()
    zeros()
    gather_b("t", xt, "x+")
    gather_b("t", xt, "x-")
    gather_b("t", xt, "y+")
    gather_b("t", xt, "y-")
    weights_step(0, 1, "z+")
    weights_step(0, 1, "z-")
    gather_b("c", xc, "x+")
    gather_b("c", xc, "x-")
    gather_b("c", xc, "y+")
    weights_step(1, 1, "z+")
    weights_step(1, 1, "z-")
    gather_b("c", xc, "y-")
    weights_step(2, 1, "z+")
    weights_step(2, 1, "z-")
    gather_c1("t", xt)
    gather_c2("t", xt)
    weights_step(0, 2, "z+")
    weights_step(0, 2, "z-")
    weights_step(1, 2, "z+")
    weights_step(1, 2, "z-")
    weights_step(2, 2, "z+")
    weights_step(2, 2, "z-")
    gather_d("t", xt, "y+")
    gather_d("t", xt, "y-")
    weights_step(0, 3, "z+")
    gather_d("t", xt, "x+")
    gather_d("t", xt, "x-")
    weights_step(0, 3, "z-")
    gather_c1("c", xc)
    gather_c2("c", xc)
    weights_step(1, 3, "z+")
    weights_step(1, 3, "z-")
    weights_step(2, 3, "z+")
    weights_step(2, 3, "z-")
    weights_far(0)
    weights_end(0)
    weights_far(1)
    weights_end(1)
    gather_end("t")
    panels(forward, 0, 2)
    weights_far(2)
    panels(forward, 2, 4)
    weights_end(2)
    panels(spread_out, 0, 2)
    panels(spread_out, 2, 4)
    gather_d("c", xc, "x+")
    gather_d("c", xc, "x-")
    gather_d("c", xc, "y+")
    gather_d("c", xc, "y-")
    panels(forward, 4, 6)
    panels(spread_out, 4, 6)
    panels(forward, 6, 8)
    panels(spread_out, 6, 8)
    collect(b_out, s_out, T_LAST_OUT)
    o_y1[0]()
    o_x1[0]()
    turn_some(0, 16)
    turn_some(16, 32)
    gather_end("c")
    panels(deltas, 0, 2)
    panels(deltas, 2, 4)
    panels(deltas, 4, 6)
    panels(deltas, 6, 8)
    panels(terms, 0, 1)
    sibling(4)
    o_y1[1]("+")
    o_y1[1]("-")
    o_x1[1]("+")
    o_x1[1]("-")
    panels(backward, 0, 2)
    pair_sum(4)
    z_send("z+", 1, 0)
    z_send("z-", 1, 1)
    panels(backward, 2, 4)
    panels(backward, 4, 6)
    panels(backward, 6, 8)
    collect(b_in, s_in, T_LAST_IN)
    i_y1[0]()
    i_x1[0]()
    panels(terms, 1, 3)
    sibling(3)
    sibling(-3)
    o_y1[2]()
    o_x2[0]()
    o_x1[2]()
    pair_sum(3)
    z_send("z+", 2, 0)
    z_send("z+", 2, 1)
    pair_sum(-3)
    z_send("z-", 2, 1)
    z_send("z-", 2, 0)
    o_y2[0]()
    panels(terms, 3, 5)
    sibling(2)
    sibling(-2)
    i_y1[1]("+")
    i_y1[1]("-")
    i_x1[1]("+")
    i_x1[1]("-")
    panels(terms, 5, 7)
    sibling(1)
    sibling(-1)
    pair_sum(2)
    z_send("z+", 3, 0)
    pair_sum(-2)
    z_send("z-", 3, 1)
    o_x2[1]("+")
    o_x2[1]("-")
    pair_sum(1)
    o_y2[1]("+")
    pair_sum(-1)
    o_y2[1]("-")
    panels(terms, 7, 8)
    sibling(0)
    z_send("z+", 3, 1)
    z_send("z-", 3, 0)
    pair_sum(0)
    i_y1[2]()
    i_x2[0]()
    i_x1[2]()
    z_send("z+", 4, 0)
    i_y2[0]()
    z_send("z-", 4, 1)
    o_x2[2]()
    o_y2[2]()
    write_out(out_ref, b_out)
    z_send("z+", 4, 1)
    z_send("z-", 4, 0)
    i_x2[1]("+")
    i_x2[1]("-")
    i_y2[1]("+")
    i_y2[1]("-")
    i_x2[2]()
    i_y2[2]()
    write_out(in_ref, b_in)
    z_last(1)
    z_last(0)
    cp.recv(("gf", 1))
    cp.recv(("gf", 0))
    cp.finish()


def finish(out, in_grad, grads, out_, in_grad_, gate, up, down, sems):
    pairs = [(out, out_), (in_grad, in_grad_)]
    pairs += [(grads.at[i], ref.at[0]) for i, ref in enumerate((gate, up, down))]
    copies = [pltpu.make_async_copy(*pair, sems.at[i]) for i, pair in enumerate(pairs)]
    for copy in copies:
        copy.start()
    for copy in copies:
        copy.wait()


def per_device(
    tokens, cotangent, gate_blocks, up_blocks, down_blocks, gate_index, up_index, down_index
):
    hbm_spec = pl.BlockSpec(memory_space=pltpu.HBM)
    vmem_spec = pl.BlockSpec(memory_space=pltpu.VMEM)
    grad = jax.ShapeDtypeStruct((1, SLOTS, BLK, BLK), F32)
    act = jax.ShapeDtypeStruct((128, 4 * BLK), BF16)
    big = (4, 4, 2, 256, BLK)
    count = 190
    results = pl.pallas_call(
        kernel,
        out_shape=(act, act, jax.ShapeDtypeStruct((3, SLOTS, BLK, BLK), F32)),
        in_specs=[hbm_spec] * 8,
        out_specs=(vmem_spec,) * 3,
        scratch_shapes=[
            pltpu.VMEM((3, SLOTS, BLK), I32),
            pltpu.VMEM((T_ROWS, BLK), I32),
            pltpu.SMEM((T_ROWS, BLK), I32),
            pltpu.VMEM((5, 4, 2, 256, BLK), BF16),
            pltpu.VMEM((5, 4, 2, 256, BLK), BF16),
            pltpu.VMEM((5, 4, 2, BLK, 256), BF16),
            pltpu.VMEM((3, GROUP, SLOTS, BLK, BLK), BF16),
            pltpu.VMEM((NBLK + 1, 256, BLK), F32),
            pltpu.VMEM((2 * NBLK + 1, 256, BLK), F32),
            pltpu.VMEM((GROUP, 256, BLK), BF16),
            pltpu.VMEM((GROUP, 256, BLK), BF16),
            pltpu.VMEM((GROUP, 256, BLK), BF16),
            pltpu.VMEM((GROUP, 256, BLK), F32),
            pltpu.VMEM((GROUP, 256, BLK), F32),
            pltpu.VMEM(big, BF16),
            pltpu.VMEM(big, BF16),
            pltpu.VMEM((3, GROUP, SLOTS, BLK, BLK), BF16),
            pltpu.VMEM((2, 3, 2, 2, 256, BLK), BF16),
            pltpu.VMEM((2, 3, 2, 4, 128, BLK), BF16),
            pltpu.VMEM((2, 3, 2, 128, BLK), BF16),
            pltpu.VMEM((2, 3, 2, 128, BLK), BF16),
            pltpu.VMEM((3, GROUP, 2, BLK, BLK), BF16),
            pltpu.VMEM((2, 4, 2, 3, BLK, BLK), BF16),
            pltpu.SemaphoreType.DMA((1,)),
            pltpu.SemaphoreType.DMA((14,)),
            pltpu.SemaphoreType.DMA((count,)),
            pltpu.SemaphoreType.DMA((count,)),
        ],
        compiler_params=pltpu.CompilerParams(
            collective_id=0, has_side_effects=True, vmem_limit_bytes=60 << 20
        ),
        name="ffn",
    )(gate_index.T, up_index.T, down_index.T, tokens, cotangent, gate_blocks, up_blocks, down_blocks)
    return pl.pallas_call(
        finish,
        out_shape=(act, act, grad, grad, grad),
        in_specs=[vmem_spec] * 3,
        out_specs=(hbm_spec,) * 5,
        scratch_shapes=[pltpu.SemaphoreType.DMA((5,))],
        name="results",
    )(*results)


def solution(mesh):
    act = P(("dp", "col"), "row")
    blocks = P(("row", "col"), None, None, None)
    return jax.shard_map(
        per_device,
        mesh=mesh,
        in_specs=(act, act, blocks, blocks, blocks, P(), P(), P()),
        out_specs=(act, act, blocks, blocks, blocks),
        check_vma=False,
    )
```

```python
import jax
import jax.numpy as jnp
from jax import lax
from jax.experimental import pallas as pl
from jax.experimental.pallas import tpu as pltpu
from jax.sharding import PartitionSpec as P

BLK = 128
SLOTS = 4
GROUP = 8
NBLK = 32
SENDS, RECVS = 40, 72
F32 = jnp.float32
BF16 = jnp.bfloat16
MESH = pl.DeviceIdType.MESH

T_GATE, T_UP, T_DOWN, T_PREV_OUT, T_PREV_GATE, T_PREV_UP, T_LAST_OUT, T_LAST_IN = 0, 4, 8, 12, 16, 20, 24, 56
T_ROWS = 88
I32 = jnp.int32


def dot(a, b, dims):
    return lax.dot_general(a, b, (dims, ((), ())), preferred_element_type=F32)


def block_of(ref, place):
    return ref[place // 8, (place // 2) % 4, place % 2]


class Copies:
    def __init__(self, send_sem, recv_sem, neighbours, back):
        self.send_sem, self.recv_sem, self.neighbours, self.back = send_sem, recv_sem, neighbours, back
        self.made, self.used, self.clock, self.recv_count = {}, [], 0, 0

    def free(self, way):
        heard = max(
            (m["sent"] for m in self.made.values() if m["way"] == self.back.get(way, way) and m["got"]),
            default=-1,
        )
        for m in self.made.values():
            if m["way"] == way and m["held"] and m["got"] and m["got"] < heard:
                m["held"] = False
                return m["number"]
        self.recv_count += 1
        return self.recv_count - 1

    def send(self, name, src, dst, way):
        self.clock += 1
        number = self.free(way)
        if len(self.used) < SENDS:
            slot = len(self.used)
        else:
            slot, earlier = self.used[-SENDS]
            earlier.wait_send()
        copy = pltpu.make_async_remote_copy(
            src_ref=src,
            dst_ref=dst,
            send_sem=self.send_sem.at[slot],
            recv_sem=self.recv_sem.at[number],
            device_id=self.neighbours[way],
            device_id_type=MESH,
        )
        copy.start()
        self.used.append((slot, copy))
        self.made[name] = {
            "copy": copy, "way": way, "number": number, "sent": self.clock, "got": 0, "held": True,
        }

    def recv(self, name):
        self.clock += 1
        self.made[name]["copy"].wait_recv()
        self.made[name]["got"] = self.clock

    def finish(self):
        assert self.recv_count <= RECVS, self.recv_count
        for _, copy in self.used[-SENDS:]:
            copy.wait_send()


def add_into(dst, srcs, dims, rows=64):
    total = 1
    for size in dims[:-2]:
        total *= size
    per = dims[-2] // rows

    def body(i, _):
        index = []
        rest = i // per
        for size in reversed(dims[:-2]):
            index.insert(0, rest % size)
            rest = rest // size
        index = tuple(index) + (pl.ds(pl.multiple_of((i % per) * rows, rows), rows),)
        value = dst[index].astype(F32)
        for src in srcs:
            value = value + src[index].astype(F32)
        dst[index] = value.astype(dst.dtype)
        return 0

    lax.fori_loop(0, total * per, body, 0)


def make_table(keys, tab, first):
    lane = lax.broadcasted_iota(I32, (SLOTS, BLK), 1)
    panel = lane & 7

    def place(v):
        return jnp.where(v < NBLK, (v & 3) * 8 + (v >> 2), NBLK)

    gate, up, down = (place(keys[i]) for i in range(3))
    tab[T_GATE:T_GATE + SLOTS] = gate
    tab[T_UP:T_UP + SLOTS] = up
    tab[T_DOWN:T_DOWN + SLOTS] = down

    prev_out = jnp.full((SLOTS, BLK), NBLK, I32)
    prev_gate = jnp.full((SLOTS, BLK), 2 * NBLK, I32)
    prev_up = prev_gate
    for d in range(GROUP - 1, -1, -1):
        far = panel >= d
        if d:
            moved = pltpu.roll(down, d, axis=1)
            for s in range(SLOTS):
                hit = (down == moved[s:s + 1]) & far
                prev_out = jnp.where(hit, (panel - d) * SLOTS + s, prev_out)
        for i, src in enumerate((gate, up)):
            if d == 0 and i == 1:
                continue
            moved = pltpu.roll(src, d, axis=1) if d else src
            for s in range(SLOTS):
                number = (panel - d) * 8 + i * SLOTS + s
                if d:
                    prev_gate = jnp.where((gate == moved[s:s + 1]) & far, number, prev_gate)
                prev_up = jnp.where((up == moved[s:s + 1]) & far, number, prev_up)
    tab[T_PREV_OUT:T_PREV_OUT + SLOTS] = prev_out
    tab[T_PREV_GATE:T_PREV_GATE + SLOTS] = prev_gate
    tab[T_PREV_UP:T_PREV_UP + SLOTS] = prev_up

    wanted = lax.broadcasted_iota(I32, (NBLK, BLK), 0)
    ours = lax.broadcasted_iota(I32, (NBLK, BLK), 1) - first
    inside = (ours >= 0) & (ours < GROUP)

    def last(sources, per):
        best = jnp.full((NBLK, BLK), -1, I32)
        for i, src in enumerate(sources):
            for s in range(SLOTS):
                hit = (wanted == src[s:s + 1]) & inside
                best = jnp.maximum(best, jnp.where(hit, ours * per + i * SLOTS + s, -1))
        best = jnp.max(best, axis=1, keepdims=True)
        best = jnp.where(best < 0, per * GROUP, best)
        return jnp.broadcast_to(best, (NBLK, BLK))

    tab[T_LAST_OUT:T_LAST_OUT + NBLK] = last((down,), SLOTS)
    tab[T_LAST_IN:T_LAST_IN + NBLK] = last((gate, up), 2 * SLOTS)


def kernel(
    gate_index, up_index, down_index, tokens, cotangent, gate_blocks, up_blocks, down_blocks,
    out_ref, in_ref, grad_ref,
    keys, tab, table, xt, xc, turned, w, s_out, s_in, act_s, gd_s, ud_s, swish_s, slope_s,
    b_out, b_in, grads, ra, rb, qa, qb, g_sib, rz,
    key_sem, local_sem, send_sem, recv_sem,
):
    core = lax.axis_index("dp")
    row = lax.axis_index("row")
    col = lax.axis_index("col")
    y, xh, xl, z = row // 2, row % 2, col // 8, col % 8
    x = xh * 2 + xl

    def at(core=core, x=x, y=y, z=z):
        return (core, y * 2 + x // 2, (x % 2) * 8 + z)

    xs = [(x + o) % 4 for o in range(4)]
    ys = [(y + o) % 4 for o in range(4)]
    zs = [(z + o) % 8 for o in range(8)]
    ways = {
        "x+": at(x=xs[1]), "x-": at(x=xs[3]), "y+": at(y=ys[1]), "y-": at(y=ys[3]),
        "z+": at(z=zs[1]), "z-": at(z=zs[7]), "c": at(core=1 - core),
    }
    yp, yl = y // 2, y % 2
    met = list(ways.values()) + [at(x=xs[2]), at(y=ys[2])]
    ways.update({
        ("x", 0): at(x=(1 - xh) * 2 + xl), ("x", 1): at(x=(1 - xh) * 2 + 1 - xl),
        ("x", 2): at(x=xh * 2 + 1 - xl), ("y", 0): at(y=(1 - yp) * 2 + yl),
        ("y", 1): at(y=(1 - yp) * 2 + 1 - yl), ("y", 2): at(y=yp * 2 + 1 - yl),
    })
    back = {"x+": "x-", "x-": "x+", "y+": "y-", "y-": "y+", "z+": "z-", "z-": "z+"}
    cp = Copies(send_sem, recv_sem, ways, back)

    barrier = pltpu.get_barrier_semaphore()
    for device in met:
        pl.semaphore_signal(barrier, inc=1, device_id=device, device_id_type=MESH)

    def half(x_):
        return pl.ds(pl.multiple_of((x_ % 2) * 128, 128), 128)

    local = {}

    def copy_in(name, src, dst):
        copy = pltpu.make_async_copy(src, dst, local_sem.at[len(local)])
        copy.start()
        local[name] = copy

    for t, src, dst in (("t", tokens, xt), ("c", cotangent, xc)):
        for hj in range(4):
            copy_in((t, hj), src.at[:, pl.ds(hj * BLK, BLK)], dst.at[hj, y, xh, half(x)])
    for i, src in enumerate((gate_blocks, up_blocks, down_blocks)):
        copy_in(("w", i), src.at[0], w.at[i, z])
    for i, src in enumerate((gate_index, up_index, down_index)):
        copy_in(("k", i), src, keys.at[i])
    pl.semaphore_wait(barrier, len(met))

    def landed(name, count):
        for i in range(count):
            local[name, i].wait()

    def piece(ref, hj, n, y_, x_):
        return ref.at[pl.ds(hj, n), y_, x_ // 2, half(x_)]

    def line_x(ref, hj, y_):
        return ref.at[hj, y_]

    def line_y(ref, hj, x_):
        return ref.at[hj, :, x_ // 2, half(x_)]

    def send_same(name, ref, way):
        cp.send(name, ref, ref, way)

    def gather_a(t, ref, src):
        for hj, way in ((0, "x+"), (1, "x-"), (2, "y+"), (3, "y-"), (1, "x+"), (0, "x-"), (3, "y+"), (2, "y-")):
            cp.send(
                (t, "a", way, hj), src.at[:, pl.ds(hj * BLK, BLK)], ref.at[hj, y, xh, half(x)], way
            )

    def gather_b(t, ref, way):
        hj, y_, x_ = {
            "x+": (0, y, xs[3]), "x-": (1, y, xs[1]), "y+": (2, ys[3], x), "y-": (3, ys[1], x),
        }[way]
        cp.recv((t, "a", way, hj))
        send_same((t, "b", way), piece(ref, hj, 1, y_, x_), way)

    def gather_c1(t, ref):
        cp.recv((t, "a", "x+", 1))
        cp.recv((t, "a", "x-", 0))
        cp.recv((t, "b", "x+"))
        cp.recv((t, "b", "x-"))
        for hj, way in ((0, "y+"), (1, "y-"), (1, "y+"), (0, "y-")):
            send_same((t, "c", way, hj), line_x(ref, hj, y), way)

    def gather_c2(t, ref):
        cp.recv((t, "a", "y+", 3))
        cp.recv((t, "a", "y-", 2))
        cp.recv((t, "b", "y+"))
        cp.recv((t, "b", "y-"))
        for hj, way in ((2, "x+"), (3, "x-"), (3, "x+"), (2, "x-")):
            send_same((t, "c", way, hj), line_y(ref, hj, x), way)

    def gather_d(t, ref, way):
        hj = {"y+": 0, "y-": 1, "x+": 2, "x-": 3}[way]
        cp.recv((t, "c", way, hj))
        part = {
            "y+": line_x(ref, 0, ys[3]), "y-": line_x(ref, 1, ys[1]),
            "x+": line_y(ref, 2, xs[3]), "x-": line_y(ref, 3, xs[1]),
        }[way]
        send_same((t, "d", way), part, way)

    def gather_end(t):
        for hj, way in ((1, "y+"), (0, "y-"), (3, "x+"), (2, "x-")):
            cp.recv((t, "c", way, hj))
        for way in ("y+", "y-", "x+", "x-"):
            cp.recv((t, "d", way))

    mine = core * 2

    def w_piece(i, o, first=0, n=2):
        return w.at[i, zs[o % 8], pl.ds(mine + first, n)]

    def weights_first(i):
        src = (gate_blocks, up_blocks, down_blocks)[i].at[0, pl.ds(mine, 2)]
        for way in ("z+", "z-"):
            cp.send(("w", i, 1, way), src, w_piece(i, 0), way)

    def weights_step(i, k, way):
        o, first = (-k, 0) if way == "z+" else (k, 1)
        cp.recv(("w", i, k, way))
        if k < 3:
            send_same(("w", i, k + 1, way), w_piece(i, o), way)
        else:
            send_same(("w", i, 4, way), w_piece(i, o, first, 1), way)
        send_same(("ws", i, -o), w_piece(i, o), "c")

    def weights_far(i):
        cp.recv(("w", i, 4, "z+"))
        cp.recv(("w", i, 4, "z-"))
        send_same(("ws", i, 4), w_piece(i, 4), "c")

    def weights_end(i, k):
        cp.recv(("ws", i, k))
        if k < 4:
            cp.recv(("ws", i, -k))

    line = (row * 2 + xl) * GROUP
    def picked(ref, first, p, axis=1):
        return jnp.concatenate(
            [block_of(ref, table[first + s, line + p]) for s in range(SLOTS)], axis=axis
        )

    def w_rows(i, p):
        return w[i, p].reshape(SLOTS * BLK, BLK)

    def w_lanes(i, p):
        return jnp.concatenate([w[i, p, s] for s in range(SLOTS)], axis=1)

    def forward(j, _):
        p = (z + 8 + ((j + 1) // 2) * (2 * (j % 2) - 1)) % GROUP
        gate = dot(picked(xt, T_GATE, p), w_rows(0, p), ((1,), (0,)))
        up = dot(picked(xt, T_UP, p), w_rows(1, p), ((1,), (0,)))
        sig = jax.nn.sigmoid(gate)
        swish = gate * sig
        act = (swish * up).astype(BF16)
        act_s[p] = act
        swish_s[p] = swish
        slope_s[p] = up * (sig * (1.0 + gate * (1.0 - sig)))
        return 0

    def spread_out(p, _):
        before = [s_out[table[T_PREV_OUT + s, line + p]] for s in range(SLOTS)]
        spread = dot(act_s[p], w_lanes(2, p), ((1,), (0,)))
        for s in range(SLOTS):
            s_out[p * SLOTS + s] = before[s] + spread[:, s * BLK:(s + 1) * BLK]
        return 0

    def deltas(p, _):
        act_grad = dot(picked(xc, T_DOWN, p), w_lanes(2, p), ((1,), (1,)))
        gd_s[p] = (act_grad * slope_s[p]).astype(BF16)
        ud_s[p] = (act_grad * swish_s[p]).astype(BF16)
        return 0

    def backward(p, _):
        for i, delta, first in ((0, gd_s, T_PREV_GATE), (1, ud_s, T_PREV_UP)):
            before = [s_in[table[first + s, line + p]] for s in range(SLOTS)]
            back = dot(delta[p], w_rows(i, p), ((1,), (1,)))
            for s in range(SLOTS):
                s_in[p * 8 + i * SLOTS + s] = before[s] + back[:, s * BLK:(s + 1) * BLK]
        return 0

    def terms(j, _):
        odd = j % 2
        p = (z + 4 + (j // 2) * (1 - odd) - ((j + 1) // 2) * odd) % GROUP
        term = dot(act_s[p], picked(xc, T_DOWN, p), ((0,), (0,)))
        for s in range(SLOTS):
            grads[2, p, s] = term[:, s * BLK:(s + 1) * BLK].astype(BF16)
        for i, first, delta in ((0, T_GATE, gd_s), (1, T_UP, ud_s)):
            term = dot(picked(turned, first, p, axis=0), delta[p], ((1,), (0,)))
            grads[i, p] = term.astype(BF16).reshape(SLOTS, BLK, BLK)
        return 0

    def turn(q, _):
        turned[q // 8, (q // 2) % 4, q % 2] = xt[q // 8, (q // 2) % 4, q % 2].T
        return 0

    def panels(body, lower=0, upper=GROUP):
        lax.fori_loop(lower, upper, body, 0)

    def collect(dst, src, first):
        def body(q, _):
            dst[q // 8, (q // 2) % 4, q % 2] = src[table[first + q, 0]].astype(BF16)
            return 0

        lax.fori_loop(0, NBLK, body, 0)

    def stage(t, name, axis, hj, part, bufs, cut, dims, halves):
        near = xs if axis == "x" else ys
        plus, minus = axis + "+", axis + "-"
        b1, b2, b3 = bufs

        def first():
            for n, far, mid in ((1, 2, (0, 1)), (2, 0, (1, 0))):
                for h in range(halves):
                    for d, way in enumerate((plus, minus)):
                        there = near[2] if n == 1 else near[(1, 3)[d]]
                        buf = (b1, b2)[n - 1].at[d]
                        cp.send((t, name, n, way, h), cut(part(hj + mid[d], there), h), cut(buf, h), way)

        def second(sign, h):
            way, part_, d = (
                (plus, part(hj, near[1]), 0) if sign == "+" else (minus, part(hj + 1, near[3]), 1)
            )
            cp.recv((t, name, 1, way, h))
            add_into(cut(part_, h), [cut(b1.at[d], h)], dims)
            cp.send((t, name, 3, way, h), cut(part_, h), cut(b3.at[d], h), way)

        def third(h):
            cp.recv((t, name, 2, plus, h))
            cp.recv((t, name, 2, minus, h))
            cp.recv((t, name, 3, plus, h))
            add_into(cut(part(hj, near[0]), h), [cut(b3.at[0], h), cut(b2.at[1], h)], dims)
            cp.recv((t, name, 3, minus, h))
            add_into(cut(part(hj + 1, near[0]), h), [cut(b2.at[0], h), cut(b3.at[1], h)], dims)

        return first, second, third

    def direct(t, name, axis, part, buf):
        def first(h):
            for n in ((0, 1), (2,))[h]:
                cp.send((t, name, n), part(n), buf.at[n], (axis, n))

        def last():
            for n in range(3):
                cp.recv((t, name, n))
            add_into(part(3), [buf.at[n] for n in range(3)], (2, 128, BLK))

        return first, last

    def reduce_of(k, t, ref):
        def along_x(hj, y_):
            return ref.at[hj, y_]

        def along_y(hj, x_):
            return ref.at[hj, :, x_ // 2, half(x_)]

        def end_x(n):
            xh_, xl_ = (1 - xh if n < 2 else xh), (xl if n in (0, 3) else 1 - xl)
            return ref.at[pl.ds(0, 2), y, xh_, half(xl_)]

        def end_y(n):
            yp_, yl_ = (1 - yp if n < 2 else yp), (yl if n in (0, 3) else 1 - yl)
            return ref.at[pl.ds(2, 2), yp_ * 2 + yl_, xh, half(x)]

        halves = 1 + k

        def cut_x(part, h):
            return part.at[xh if h else 1 - xh] if k else part

        def cut_y(part, h):
            return part.at[pl.ds((yp if h else 1 - yp) * 2, 2)] if k else part

        dims = ((2, 256, BLK), (4, 128, BLK)) if k == 0 else ((256, BLK), (2, 128, BLK))

        y1 = stage(t, "y1", "y", 0, along_x, [ra.at[k, i] for i in range(3)], cut_x, dims[0], halves)
        x1 = stage(t, "x1", "x", 2, along_y, [rb.at[k, i] for i in range(3)], cut_y, dims[1], halves)
        x2 = direct(t, "x2", "x", end_x, qa.at[k])
        y2 = direct(t, "y2", "y", end_y, qb.at[k])
        return y1, x1, x2, y2

    o_y1, o_x1, o_x2, o_y2 = reduce_of(0, "o", b_out)
    i_y1, i_x1, i_x2, i_y2 = reduce_of(1, "i", b_in)

    theirs = (1 - core) * 2

    def sibling(o):
        p = zs[o % 8]
        cp.send(("gs", o), grads.at[:, p, pl.ds(theirs, 2)], g_sib.at[:, p], "c")

    def pair_sum(o):
        cp.recv(("gs", o))
        p = zs[o % 8]
        add_into(grads.at[:, p, pl.ds(mine, 2)], [g_sib.at[:, p]], (3, 2, 128, BLK))

    def z_send(way, k, s):
        d, sign, begins = (0, 1, 0) if way == "z+" else (1, -1, 1)
        for i, n in ((2, 1), (0, 2)):
            part = grads.at[pl.ds(i, n), zs[sign * (5 - k) % 8], mine + s]
            if k > 2 or (k == 2 and s == begins):
                cp.recv(("z", way, k - 1, s, i))
                add_into(part, [rz.at[d, k - 2, s, pl.ds(i, n)]], (n, 128, BLK))
            cp.send(("z", way, k, s, i), part, rz.at[d, k - 1, s, pl.ds(i, n)], way)

    def z_last(s):
        for i in (2, 0):
            cp.recv(("z", "z+", 4, s, i))
            cp.recv(("z", "z-", 4, s, i))

        def body(n, _):
            rows = pl.ds(pl.multiple_of((n % 2) * 64, 64), 64)
            i = n // 2
            grad_ref[i, mine + s, rows] = (
                grads[i, z, mine + s, rows].astype(F32)
                + rz[0, 3, s, i, rows].astype(F32)
                + rz[1, 3, s, i, rows].astype(F32)
            )
            return 0

        lax.fori_loop(0, 6, body, 0)
        part = grad_ref.at[:, mine + s]
        cp.send(("gf", s), part, part, "c")

    table_copy = pltpu.make_async_copy(tab, table, key_sem.at[0])

    def table_start():
        landed("k", 3)
        make_table(keys, tab, line)
        table_copy.start()

    def zeros():
        for ref in (xt, xc):
            ref[4, 0, 0] = jnp.zeros((256, BLK), BF16)
        turned[4, 0, 0] = jnp.zeros((BLK, 256), BF16)
        s_out[NBLK] = jnp.zeros((256, BLK), F32)
        s_in[2 * NBLK] = jnp.zeros((256, BLK), F32)

    def turn_some(lower, upper):
        lax.fori_loop(lower, upper, turn, 0)

    def write_out(ref, b):
        for hj in range(4):
            ref[:, hj * BLK:(hj + 1) * BLK] = b[hj, y, xh, half(x)]

    gather_a("t", xt, tokens)
    weights_first(0)
    weights_first(1)
    gather_a("c", xc, cotangent)
    weights_first(2)
    table_start()
    landed("t", 4)
    landed("w", 3)
    landed("c", 4)
    table_copy.wait()
    zeros()
    gather_b("t", xt, "x+")
    gather_b("t", xt, "x-")
    gather_b("t", xt, "y+")
    gather_b("t", xt, "y-")
    gather_b("c", xc, "x+")
    gather_b("c", xc, "x-")
    gather_b("c", xc, "y+")
    gather_b("c", xc, "y-")
    weights_step(0, 1, "z+")
    weights_step(0, 1, "z-")
    weights_end(0, 1)
    gather_c1("t", xt)
    gather_c2("t", xt)
    weights_step(1, 1, "z+")
    weights_step(1, 1, "z-")
    weights_step(2, 1, "z+")
    weights_step(2, 1, "z-")
    weights_end(1, 1)
    weights_end(2, 1)
    weights_step(0, 2, "z+")
    weights_step(0, 2, "z-")
    weights_end(0, 2)
    weights_step(1, 2, "z+")
    weights_step(1, 2, "z-")
    gather_d("t", xt, "y+")
    gather_d("t", xt, "y-")
    gather_c1("c", xc)
    gather_d("t", xt, "x+")
    gather_d("t", xt, "x-")
    gather_c2("c", xc)
    weights_end(1, 2)
    weights_step(2, 2, "z+")
    weights_step(2, 2, "z-")
    weights_end(2, 2)
    weights_step(0, 3, "z+")
    weights_step(0, 3, "z-")
    weights_end(0, 3)
    weights_step(1, 3, "z+")
    weights_step(1, 3, "z-")
    weights_end(1, 3)
    weights_step(2, 3, "z+")
    gather_end("t")
    weights_step(2, 3, "z-")
    panels(forward, 0, 1)
    weights_far(0)
    panels(forward, 1, 3)
    weights_end(2, 3)
    panels(forward, 3, 5)
    weights_end(0, 4)
    weights_far(1)
    panels(forward, 5, 7)
    gather_d("c", xc, "x+")
    gather_d("c", xc, "x-")
    gather_d("c", xc, "y+")
    gather_d("c", xc, "y-")
    weights_end(1, 4)
    panels(forward, 7, 8)
    turn_some(0, 16)
    weights_far(2)
    turn_some(16, 32)
    weights_end(2, 4)
    panels(spread_out, 0, 2)
    panels(spread_out, 2, 4)
    panels(spread_out, 4, 6)
    panels(spread_out, 6, 8)
    gather_end("c")
    collect(b_out, s_out, T_LAST_OUT)
    o_y1[0]()
    o_x1[0]()
    panels(deltas, 0, 2)
    panels(deltas, 2, 4)
    panels(deltas, 4, 6)
    panels(deltas, 6, 8)
    panels(terms, 0, 1)
    sibling(4)
    panels(terms, 1, 3)
    sibling(3)
    sibling(-3)
    panels(backward, 0, 2)
    pair_sum(4)
    z_send("z+", 1, 0)
    z_send("z-", 1, 1)
    pair_sum(3)
    z_send("z+", 2, 1)
    pair_sum(-3)
    z_send("z-", 2, 0)
    o_y1[1]("+", 0)
    o_y1[1]("-", 0)
    o_x1[1]("+", 0)
    o_x1[1]("-", 0)
    panels(backward, 2, 4)
    panels(backward, 4, 6)
    panels(backward, 6, 8)
    collect(b_in, s_in, T_LAST_IN)
    i_y1[0]()
    i_x1[0]()
    z_send("z+", 2, 0)
    z_send("z-", 2, 1)
    panels(terms, 3, 5)
    sibling(2)
    sibling(-2)
    o_y1[2](0)
    o_x2[0](0)
    o_x2[0](1)
    o_x1[2](0)
    pair_sum(2)
    z_send("z+", 3, 1)
    pair_sum(-2)
    z_send("z-", 3, 0)
    i_y1[1]("+", 0)
    i_y1[1]("-", 0)
    i_x1[1]("+", 0)
    i_x1[1]("-", 0)
    i_y1[1]("+", 1)
    i_y1[1]("-", 1)
    o_y2[0](0)
    i_x1[1]("+", 1)
    i_x1[1]("-", 1)
    z_send("z+", 3, 0)
    z_send("z-", 3, 1)
    o_y2[0](1)
    panels(terms, 5, 7)
    sibling(1)
    sibling(-1)
    panels(terms, 7, 8)
    sibling(0)
    pair_sum(1)
    z_send("z+", 4, 1)
    pair_sum(-1)
    z_send("z-", 4, 0)
    pair_sum(0)
    i_y1[2](0)
    i_x2[0](0)
    i_y1[2](1)
    i_x2[0](1)
    z_send("z+", 4, 0)
    z_send("z-", 4, 1)
    o_x2[1]()
    i_x1[2](0)
    i_y2[0](0)
    o_y2[1]()
    write_out(out_ref, b_out)
    i_x1[2](1)
    i_y2[0](1)
    z_last(0)
    z_last(1)
    i_x2[1]()
    i_y2[1]()
    write_out(in_ref, b_in)
    cp.recv(("gf", 0))
    cp.recv(("gf", 1))
    cp.finish()


def finish(out, in_grad, grads, out_, in_grad_, gate, up, down, sems):
    pairs = [(out, out_), (in_grad, in_grad_)]
    pairs += [(grads.at[i], ref.at[0]) for i, ref in enumerate((gate, up, down))]
    copies = [pltpu.make_async_copy(*pair, sems.at[i]) for i, pair in enumerate(pairs)]
    for copy in copies:
        copy.start()
    for copy in copies:
        copy.wait()


def per_device(
    tokens, cotangent, gate_blocks, up_blocks, down_blocks, gate_index, up_index, down_index
):
    hbm_spec = pl.BlockSpec(memory_space=pltpu.HBM)
    vmem_spec = pl.BlockSpec(memory_space=pltpu.VMEM)
    grad = jax.ShapeDtypeStruct((1, SLOTS, BLK, BLK), F32)
    act = jax.ShapeDtypeStruct((128, 4 * BLK), BF16)
    big = (4, 4, 2, 256, BLK)
    results = pl.pallas_call(
        kernel,
        out_shape=(act, act, jax.ShapeDtypeStruct((3, SLOTS, BLK, BLK), F32)),
        in_specs=[hbm_spec] * 8,
        out_specs=(vmem_spec,) * 3,
        scratch_shapes=[
            pltpu.VMEM((3, SLOTS, BLK), I32),
            pltpu.VMEM((T_ROWS, BLK), I32),
            pltpu.SMEM((T_ROWS, BLK), I32),
            pltpu.VMEM((5, 4, 2, 256, BLK), BF16),
            pltpu.VMEM((5, 4, 2, 256, BLK), BF16),
            pltpu.VMEM((5, 4, 2, BLK, 256), BF16),
            pltpu.VMEM((3, GROUP, SLOTS, BLK, BLK), BF16),
            pltpu.VMEM((NBLK + 1, 256, BLK), F32),
            pltpu.VMEM((2 * NBLK + 1, 256, BLK), F32),
            pltpu.VMEM((GROUP, 256, BLK), BF16),
            pltpu.VMEM((GROUP, 256, BLK), BF16),
            pltpu.VMEM((GROUP, 256, BLK), BF16),
            pltpu.VMEM((GROUP, 256, BLK), F32),
            pltpu.VMEM((GROUP, 256, BLK), F32),
            pltpu.VMEM(big, BF16),
            pltpu.VMEM(big, BF16),
            pltpu.VMEM((3, GROUP, SLOTS, BLK, BLK), BF16),
            pltpu.VMEM((2, 3, 2, 2, 256, BLK), BF16),
            pltpu.VMEM((2, 3, 2, 4, 128, BLK), BF16),
            pltpu.VMEM((2, 3, 2, 128, BLK), BF16),
            pltpu.VMEM((2, 3, 2, 128, BLK), BF16),
            pltpu.VMEM((3, GROUP, 2, BLK, BLK), BF16),
            pltpu.VMEM((2, 4, 2, 3, BLK, BLK), BF16),
            pltpu.SemaphoreType.DMA((1,)),
            pltpu.SemaphoreType.DMA((14,)),
            pltpu.SemaphoreType.DMA((SENDS,)),
            pltpu.SemaphoreType.DMA((RECVS,)),
        ],
        compiler_params=pltpu.CompilerParams(
            collective_id=0, has_side_effects=True, vmem_limit_bytes=60 << 20
        ),
        name="ffn",
    )(gate_index.T, up_index.T, down_index.T, tokens, cotangent, gate_blocks, up_blocks, down_blocks)
    return pl.pallas_call(
        finish,
        out_shape=(act, act, grad, grad, grad),
        in_specs=[vmem_spec] * 3,
        out_specs=(hbm_spec,) * 5,
        scratch_shapes=[pltpu.SemaphoreType.DMA((5,))],
        name="results",
    )(*results)


def solution(mesh):
    act = P(("dp", "col"), "row")
    blocks = P(("row", "col"), None, None, None)
    return jax.shard_map(
        per_device,
        mesh=mesh,
        in_specs=(act, act, blocks, blocks, blocks, P(), P(), P()),
        out_specs=(act, act, blocks, blocks, blocks),
        check_vma=False,
    )
```

```python
import jax
import jax.numpy as jnp
from jax import lax
from jax.experimental import pallas as pl
from jax.experimental.pallas import tpu as pltpu
from jax.sharding import PartitionSpec as P

BLK = 128
SLOTS = 4
GROUP = 8
NBLK = 32
SENDS, RECVS = 40, 77
F32 = jnp.float32
BF16 = jnp.bfloat16
MESH = pl.DeviceIdType.MESH

T_GATE, T_UP, T_DOWN, T_PREV_OUT, T_PREV_GATE, T_PREV_UP, T_LAST_OUT, T_LAST_IN = 0, 4, 8, 12, 16, 20, 24, 56
T_ROWS = 88
I32 = jnp.int32


def dot(a, b, dims):
    return lax.dot_general(a, b, (dims, ((), ())), preferred_element_type=F32)


def block_of(ref, place):
    return ref[place // 8, (place // 2) % 4, place % 2]


class Copies:
    def __init__(self, send_sem, recv_sem, neighbours, back):
        self.send_sem, self.recv_sem, self.neighbours, self.back = send_sem, recv_sem, neighbours, back
        self.made, self.used, self.clock, self.recv_count = {}, [], 0, 0

    def free(self, way):
        heard = max(
            (m["sent"] for m in self.made.values() if m["way"] == self.back.get(way, way) and m["got"]),
            default=-1,
        )
        for m in self.made.values():
            if m["way"] == way and m["held"] and m["got"] and m["got"] < heard:
                m["held"] = False
                return m["number"]
        self.recv_count += 1
        return self.recv_count - 1

    def send(self, name, src, dst, way):
        self.clock += 1
        number = self.free(way)
        if len(self.used) < SENDS:
            slot = len(self.used)
        else:
            slot, earlier = self.used[-SENDS]
            earlier.wait_send()
        copy = pltpu.make_async_remote_copy(
            src_ref=src,
            dst_ref=dst,
            send_sem=self.send_sem.at[slot],
            recv_sem=self.recv_sem.at[number],
            device_id=self.neighbours[way],
            device_id_type=MESH,
        )
        copy.start()
        self.used.append((slot, copy))
        self.made[name] = {
            "copy": copy, "way": way, "number": number, "sent": self.clock, "got": 0, "held": True,
        }

    def recv(self, name):
        self.clock += 1
        self.made[name]["copy"].wait_recv()
        self.made[name]["got"] = self.clock

    def finish(self):
        assert self.recv_count <= RECVS, self.recv_count
        for _, copy in self.used[-SENDS:]:
            copy.wait_send()


def add_into(dst, srcs, dims, rows=64):
    total = 1
    for size in dims[:-2]:
        total *= size
    per = dims[-2] // rows

    def body(i, _):
        index = []
        rest = i // per
        for size in reversed(dims[:-2]):
            index.insert(0, rest % size)
            rest = rest // size
        index = tuple(index) + (pl.ds(pl.multiple_of((i % per) * rows, rows), rows),)
        value = dst[index].astype(F32)
        for src in srcs:
            value = value + src[index].astype(F32)
        dst[index] = value.astype(dst.dtype)
        return 0

    lax.fori_loop(0, total * per, body, 0, unroll=2)


def make_table(keys, tab, first):
    lane = lax.broadcasted_iota(I32, (SLOTS, BLK), 1)
    panel = lane & 7

    def place(v):
        return jnp.where(v < NBLK, (v & 3) * 8 + (v >> 2), NBLK)

    gate, up, down = (place(keys[i]) for i in range(3))
    tab[T_GATE:T_GATE + SLOTS] = gate
    tab[T_UP:T_UP + SLOTS] = up
    tab[T_DOWN:T_DOWN + SLOTS] = down

    prev_out = jnp.full((SLOTS, BLK), NBLK, I32)
    prev_gate = jnp.full((SLOTS, BLK), 2 * NBLK, I32)
    prev_up = prev_gate
    for d in range(GROUP - 1, -1, -1):
        far = panel >= d
        if d:
            moved = pltpu.roll(down, d, axis=1)
            for s in range(SLOTS):
                hit = (down == moved[s:s + 1]) & far
                prev_out = jnp.where(hit, (panel - d) * SLOTS + s, prev_out)
        for i, src in enumerate((gate, up)):
            if d == 0 and i == 1:
                continue
            moved = pltpu.roll(src, d, axis=1) if d else src
            for s in range(SLOTS):
                number = (panel - d) * 8 + i * SLOTS + s
                if d:
                    prev_gate = jnp.where((gate == moved[s:s + 1]) & far, number, prev_gate)
                prev_up = jnp.where((up == moved[s:s + 1]) & far, number, prev_up)
    tab[T_PREV_OUT:T_PREV_OUT + SLOTS] = prev_out
    tab[T_PREV_GATE:T_PREV_GATE + SLOTS] = prev_gate
    tab[T_PREV_UP:T_PREV_UP + SLOTS] = prev_up

    wanted = lax.broadcasted_iota(I32, (NBLK, BLK), 0)
    ours = lax.broadcasted_iota(I32, (NBLK, BLK), 1) - first
    inside = (ours >= 0) & (ours < GROUP)

    def last(sources, per):
        best = jnp.full((NBLK, BLK), -1, I32)
        for i, src in enumerate(sources):
            for s in range(SLOTS):
                hit = (wanted == src[s:s + 1]) & inside
                best = jnp.maximum(best, jnp.where(hit, ours * per + i * SLOTS + s, -1))
        best = jnp.max(best, axis=1, keepdims=True)
        best = jnp.where(best < 0, per * GROUP, best)
        return jnp.broadcast_to(best, (NBLK, BLK))

    tab[T_LAST_OUT:T_LAST_OUT + NBLK] = last((down,), SLOTS)
    tab[T_LAST_IN:T_LAST_IN + NBLK] = last((gate, up), 2 * SLOTS)


def kernel(
    gate_index, up_index, down_index, tokens, cotangent, gate_blocks, up_blocks, down_blocks,
    out_ref, in_ref, grad_ref,
    keys, tab, table, xt, xc, turned, w, s_out, s_in, act_s, gd_s, ud_s, swish_s, slope_s,
    b_out, b_in, grads, ra, rb, qa, qb, g_sib, rz,
    key_sem, local_sem, send_sem, recv_sem,
):
    core = lax.axis_index("dp")
    row = lax.axis_index("row")
    col = lax.axis_index("col")
    y, xh, xl, z = row // 2, row % 2, col // 8, col % 8
    x = xh * 2 + xl

    def at(core=core, x=x, y=y, z=z):
        return (core, y * 2 + x // 2, (x % 2) * 8 + z)

    xs = [(x + o) % 4 for o in range(4)]
    ys = [(y + o) % 4 for o in range(4)]
    zs = [(z + o) % 8 for o in range(8)]
    ways = {
        "x+": at(x=xs[1]), "x-": at(x=xs[3]), "y+": at(y=ys[1]), "y-": at(y=ys[3]),
        "z+": at(z=zs[1]), "z-": at(z=zs[7]), "c": at(core=1 - core),
    }
    yp, yl = y // 2, y % 2
    met = list(ways.values()) + [at(x=xs[2]), at(y=ys[2])]
    ways.update({
        ("x", 0): at(x=(1 - xh) * 2 + xl), ("x", 1): at(x=(1 - xh) * 2 + 1 - xl),
        ("x", 2): at(x=xh * 2 + 1 - xl), ("y", 0): at(y=(1 - yp) * 2 + yl),
        ("y", 1): at(y=(1 - yp) * 2 + 1 - yl), ("y", 2): at(y=yp * 2 + 1 - yl),
    })
    back = {"x+": "x-", "x-": "x+", "y+": "y-", "y-": "y+", "z+": "z-", "z-": "z+"}
    cp = Copies(send_sem, recv_sem, ways, back)

    barrier = pltpu.get_barrier_semaphore()
    for device in met:
        pl.semaphore_signal(barrier, inc=1, device_id=device, device_id_type=MESH)

    def half(x_):
        return pl.ds(pl.multiple_of((x_ % 2) * 128, 128), 128)

    local = {}

    def copy_in(name, src, dst):
        copy = pltpu.make_async_copy(src, dst, local_sem.at[len(local)])
        copy.start()
        local[name] = copy

    for t, src, dst in (("t", tokens, xt), ("c", cotangent, xc)):
        for hj in range(4):
            copy_in((t, hj), src.at[:, pl.ds(hj * BLK, BLK)], dst.at[hj, y, xh, half(x)])
    for i, src in enumerate((gate_blocks, up_blocks, down_blocks)):
        copy_in(("w", i), src.at[0], w.at[i, z])
    for i, src in enumerate((gate_index, up_index, down_index)):
        copy_in(("k", i), src, keys.at[i])
    pl.semaphore_wait(barrier, len(met))

    def landed(name, count):
        for i in range(count):
            local[name, i].wait()

    def piece(ref, hj, n, y_, x_):
        return ref.at[pl.ds(hj, n), y_, x_ // 2, half(x_)]

    def line_x(ref, hj, y_):
        return ref.at[hj, y_]

    def line_y(ref, hj, x_):
        return ref.at[hj, :, x_ // 2, half(x_)]

    def send_same(name, ref, way):
        cp.send(name, ref, ref, way)

    def gather_a(t, ref, src):
        for hj, way in ((0, "x+"), (1, "x-"), (2, "y+"), (3, "y-"), (1, "x+"), (0, "x-"), (3, "y+"), (2, "y-")):
            cp.send(
                (t, "a", way, hj), src.at[:, pl.ds(hj * BLK, BLK)], ref.at[hj, y, xh, half(x)], way
            )

    def gather_b(t, ref, way):
        hj, y_, x_ = {
            "x+": (0, y, xs[3]), "x-": (1, y, xs[1]), "y+": (2, ys[3], x), "y-": (3, ys[1], x),
        }[way]
        cp.recv((t, "a", way, hj))
        send_same((t, "b", way), piece(ref, hj, 1, y_, x_), way)

    def gather_c1(t, ref):
        cp.recv((t, "a", "x+", 1))
        cp.recv((t, "a", "x-", 0))
        cp.recv((t, "b", "x+"))
        cp.recv((t, "b", "x-"))
        for hj, way in ((0, "y+"), (1, "y-"), (1, "y+"), (0, "y-")):
            send_same((t, "c", way, hj), line_x(ref, hj, y), way)

    def gather_c2(t, ref):
        cp.recv((t, "a", "y+", 3))
        cp.recv((t, "a", "y-", 2))
        cp.recv((t, "b", "y+"))
        cp.recv((t, "b", "y-"))
        for hj, way in ((2, "x+"), (3, "x-"), (3, "x+"), (2, "x-")):
            send_same((t, "c", way, hj), line_y(ref, hj, x), way)

    def gather_d(t, ref, way):
        hj = {"y+": 0, "y-": 1, "x+": 2, "x-": 3}[way]
        cp.recv((t, "c", way, hj))
        part = {
            "y+": line_x(ref, 0, ys[3]), "y-": line_x(ref, 1, ys[1]),
            "x+": line_y(ref, 2, xs[3]), "x-": line_y(ref, 3, xs[1]),
        }[way]
        send_same((t, "d", way), part, way)

    def gather_end(t):
        for hj, way in ((1, "y+"), (0, "y-"), (3, "x+"), (2, "x-")):
            cp.recv((t, "c", way, hj))
        for way in ("y+", "y-", "x+", "x-"):
            cp.recv((t, "d", way))

    mine = core * 2

    def w_piece(i, o, first=0, n=2):
        return w.at[i, zs[o % 8], pl.ds(mine + first, n)]

    def weights_first(i):
        src = (gate_blocks, up_blocks, down_blocks)[i].at[0, pl.ds(mine, 2)]
        for way in ("z+", "z-"):
            cp.send(("w", i, 1, way), src, w_piece(i, 0), way)

    def weights_step(i, k, way):
        o, first = (-k, 0) if way == "z+" else (k, 1)
        cp.recv(("w", i, k, way))
        if k < 3:
            send_same(("w", i, k + 1, way), w_piece(i, o), way)
        else:
            send_same(("w", i, 4, way), w_piece(i, o, first, 1), way)
        send_same(("ws", i, -o), w_piece(i, o), "c")

    def weights_far(i):
        cp.recv(("w", i, 4, "z+"))
        cp.recv(("w", i, 4, "z-"))
        send_same(("ws", i, 4), w_piece(i, 4), "c")

    def weights_end(i, k):
        cp.recv(("ws", i, k))
        if k < 4:
            cp.recv(("ws", i, -k))

    line = (row * 2 + xl) * GROUP
    def picked(ref, first, p, axis=1):
        return jnp.concatenate(
            [block_of(ref, table[first + s, line + p]) for s in range(SLOTS)], axis=axis
        )

    def w_rows(i, p):
        return w[i, p].reshape(SLOTS * BLK, BLK)

    def w_lanes(i, p):
        return jnp.concatenate([w[i, p, s] for s in range(SLOTS)], axis=1)

    def forward(j, _):
        p = (z + 8 + ((j + 1) // 2) * (2 * (j % 2) - 1)) % GROUP
        gate = dot(picked(xt, T_GATE, p), w_rows(0, p), ((1,), (0,)))
        up = dot(picked(xt, T_UP, p), w_rows(1, p), ((1,), (0,)))
        sig = jax.nn.sigmoid(gate)
        swish = gate * sig
        act = (swish * up).astype(BF16)
        act_s[p] = act
        swish_s[p] = swish
        slope_s[p] = up * (sig * (1.0 + gate * (1.0 - sig)))
        return 0

    def spread_out(p, _):
        before = [s_out[table[T_PREV_OUT + s, line + p]] for s in range(SLOTS)]
        spread = dot(act_s[p], w_lanes(2, p), ((1,), (0,)))
        for s in range(SLOTS):
            s_out[p * SLOTS + s] = before[s] + spread[:, s * BLK:(s + 1) * BLK]
        return 0

    def deltas(p, _):
        act_grad = dot(picked(xc, T_DOWN, p), w_lanes(2, p), ((1,), (1,)))
        gd_s[p] = (act_grad * slope_s[p]).astype(BF16)
        ud_s[p] = (act_grad * swish_s[p]).astype(BF16)
        return 0

    def backward(p, _):
        for i, delta, first in ((0, gd_s, T_PREV_GATE), (1, ud_s, T_PREV_UP)):
            before = [s_in[table[first + s, line + p]] for s in range(SLOTS)]
            back = dot(delta[p], w_rows(i, p), ((1,), (1,)))
            for s in range(SLOTS):
                s_in[p * 8 + i * SLOTS + s] = before[s] + back[:, s * BLK:(s + 1) * BLK]
        return 0

    def terms(j, _):
        odd = j % 2
        p = (z + 4 + (j // 2) * (1 - odd) - ((j + 1) // 2) * odd) % GROUP
        term = dot(act_s[p], picked(xc, T_DOWN, p), ((0,), (0,)))
        for s in range(SLOTS):
            grads[2, p, s] = term[:, s * BLK:(s + 1) * BLK].astype(BF16)
        for i, first, delta in ((0, T_GATE, gd_s), (1, T_UP, ud_s)):
            term = dot(picked(turned, first, p, axis=0), delta[p], ((1,), (0,)))
            grads[i, p] = term.astype(BF16).reshape(SLOTS, BLK, BLK)
        return 0

    def turn(q, _):
        turned[q // 8, (q // 2) % 4, q % 2] = xt[q // 8, (q // 2) % 4, q % 2].T
        return 0

    def panels(body, lower=0, upper=GROUP):
        lax.fori_loop(lower, upper, body, 0, unroll=upper - lower)

    def collect(dst, src, first):
        def body(q, _):
            dst[q // 8, (q // 2) % 4, q % 2] = src[table[first + q, 0]].astype(BF16)
            return 0

        lax.fori_loop(0, NBLK, body, 0, unroll=4)

    def stage(t, name, axis, hj, part, bufs, cut, dims, halves):
        near = xs if axis == "x" else ys
        plus, minus = axis + "+", axis + "-"
        b1, b2, b3 = bufs

        def first():
            for n, far, mid in ((1, 2, (0, 1)), (2, 0, (1, 0))):
                for h in range(halves):
                    for d, way in enumerate((plus, minus)):
                        there = near[2] if n == 1 else near[(1, 3)[d]]
                        buf = (b1, b2)[n - 1].at[d]
                        cp.send((t, name, n, way, h), cut(part(hj + mid[d], there), h), cut(buf, h), way)

        def second(sign, h):
            way, part_, d = (
                (plus, part(hj, near[1]), 0) if sign == "+" else (minus, part(hj + 1, near[3]), 1)
            )
            cp.recv((t, name, 1, way, h))
            add_into(cut(part_, h), [cut(b1.at[d], h)], dims)
            cp.send((t, name, 3, way, h), cut(part_, h), cut(b3.at[d], h), way)

        def third(h):
            cp.recv((t, name, 2, plus, h))
            cp.recv((t, name, 2, minus, h))
            cp.recv((t, name, 3, plus, h))
            add_into(cut(part(hj, near[0]), h), [cut(b3.at[0], h), cut(b2.at[1], h)], dims)
            cp.recv((t, name, 3, minus, h))
            add_into(cut(part(hj + 1, near[0]), h), [cut(b2.at[0], h), cut(b3.at[1], h)], dims)

        return first, second, third

    def direct(t, name, axis, part, buf):
        def first(h):
            for n in ((0, 1), (2,))[h]:
                cp.send((t, name, n), part(n), buf.at[n], (axis, n))

        def last():
            for n in range(3):
                cp.recv((t, name, n))
            add_into(part(3), [buf.at[n] for n in range(3)], (2, 128, BLK))

        return first, last

    def reduce_of(k, t, ref):
        def along_x(hj, y_):
            return ref.at[hj, y_]

        def along_y(hj, x_):
            return ref.at[hj, :, x_ // 2, half(x_)]

        def end_x(n):
            xh_, xl_ = (1 - xh if n < 2 else xh), (xl if n in (0, 3) else 1 - xl)
            return ref.at[pl.ds(0, 2), y, xh_, half(xl_)]

        def end_y(n):
            yp_, yl_ = (1 - yp if n < 2 else yp), (yl if n in (0, 3) else 1 - yl)
            return ref.at[pl.ds(2, 2), yp_ * 2 + yl_, xh, half(x)]

        halves = 1 + k

        def cut_x(part, h):
            return part.at[xh if h else 1 - xh] if k else part

        def cut_y(part, h):
            return part.at[pl.ds((yp if h else 1 - yp) * 2, 2)] if k else part

        dims = ((2, 256, BLK), (4, 128, BLK)) if k == 0 else ((256, BLK), (2, 128, BLK))

        y1 = stage(t, "y1", "y", 0, along_x, [ra.at[k, i] for i in range(3)], cut_x, dims[0], halves)
        x1 = stage(t, "x1", "x", 2, along_y, [rb.at[k, i] for i in range(3)], cut_y, dims[1], halves)
        x2 = direct(t, "x2", "x", end_x, qa.at[k])
        y2 = direct(t, "y2", "y", end_y, qb.at[k])
        return y1, x1, x2, y2

    o_y1, o_x1, o_x2, o_y2 = reduce_of(0, "o", b_out)
    i_y1, i_x1, i_x2, i_y2 = reduce_of(1, "i", b_in)

    theirs = (1 - core) * 2

    def sibling(o):
        p = zs[o % 8]
        cp.send(("gs", o), grads.at[:, p, pl.ds(theirs, 2)], g_sib.at[:, p], "c")

    def pair_sum(o):
        cp.recv(("gs", o))
        p = zs[o % 8]
        add_into(grads.at[:, p, pl.ds(mine, 2)], [g_sib.at[:, p]], (3, 2, 128, BLK))

    def z_send(way, k, s):
        d, sign, begins = (0, 1, 0) if way == "z+" else (1, -1, 1)
        for i, n in ((2, 1), (0, 2)):
            part = grads.at[pl.ds(i, n), zs[sign * (5 - k) % 8], mine + s]
            if k > 2 or (k == 2 and s == begins):
                cp.recv(("z", way, k - 1, s, i))
                add_into(part, [rz.at[d, k - 2, s, pl.ds(i, n)]], (n, 128, BLK))
            cp.send(("z", way, k, s, i), part, rz.at[d, k - 1, s, pl.ds(i, n)], way)

    def z_last(s):
        for i in (2, 0):
            cp.recv(("z", "z+", 4, s, i))
            cp.recv(("z", "z-", 4, s, i))

        def body(n, _):
            rows = pl.ds(pl.multiple_of((n % 2) * 64, 64), 64)
            i = n // 2
            grad_ref[i, mine + s, rows] = (
                grads[i, z, mine + s, rows].astype(F32)
                + rz[0, 3, s, i, rows].astype(F32)
                + rz[1, 3, s, i, rows].astype(F32)
            )
            return 0

        lax.fori_loop(0, 6, body, 0)
        part = grad_ref.at[:, mine + s]
        cp.send(("gf", s), part, part, "c")

    table_copy = pltpu.make_async_copy(tab, table, key_sem.at[0])

    def table_start():
        landed("k", 3)
        make_table(keys, tab, line)
        table_copy.start()

    def zeros():
        for ref in (xt, xc):
            ref[4, 0, 0] = jnp.zeros((256, BLK), BF16)
        turned[4, 0, 0] = jnp.zeros((BLK, 256), BF16)
        s_out[NBLK] = jnp.zeros((256, BLK), F32)
        s_in[2 * NBLK] = jnp.zeros((256, BLK), F32)

    def turn_some(lower, upper):
        lax.fori_loop(lower, upper, turn, 0, unroll=4)

    def write_out(ref, b):
        for hj in range(4):
            ref[:, hj * BLK:(hj + 1) * BLK] = b[hj, y, xh, half(x)]

    gather_a("t", xt, tokens)
    weights_first(0)
    weights_first(1)
    gather_a("c", xc, cotangent)
    weights_first(2)
    table_start()
    landed("t", 4)
    landed("w", 3)
    landed("c", 4)
    table_copy.wait()
    zeros()
    gather_b("t", xt, "x+")
    gather_b("t", xt, "x-")
    gather_b("t", xt, "y+")
    gather_b("t", xt, "y-")
    gather_b("c", xc, "x+")
    gather_b("c", xc, "x-")
    gather_b("c", xc, "y+")
    gather_b("c", xc, "y-")
    weights_step(0, 1, "z+")
    weights_step(0, 1, "z-")
    weights_end(0, 1)
    weights_step(1, 1, "z+")
    weights_step(1, 1, "z-")
    gather_c1("t", xt)
    gather_c2("t", xt)
    weights_end(1, 1)
    weights_step(2, 1, "z+")
    weights_step(2, 1, "z-")
    weights_end(2, 1)
    weights_step(0, 2, "z+")
    weights_step(0, 2, "z-")
    weights_end(0, 2)
    weights_step(1, 2, "z+")
    weights_step(1, 2, "z-")
    weights_end(1, 2)
    gather_d("t", xt, "y+")
    gather_d("t", xt, "y-")
    weights_step(2, 2, "z+")
    weights_step(2, 2, "z-")
    gather_d("t", xt, "x+")
    gather_d("t", xt, "x-")
    gather_c1("c", xc)
    gather_c2("c", xc)
    weights_end(2, 2)
    weights_step(0, 3, "z+")
    weights_step(0, 3, "z-")
    weights_end(0, 3)
    weights_step(1, 3, "z+")
    weights_step(1, 3, "z-")
    weights_end(1, 3)
    weights_step(2, 3, "z+")
    weights_step(2, 3, "z-")
    gather_end("t")
    weights_end(2, 3)
    panels(forward, 0, 1)
    weights_far(0)
    panels(forward, 1, 3)
    panels(forward, 3, 5)
    weights_far(1)
    weights_end(0, 4)
    panels(forward, 5, 7)
    gather_d("c", xc, "x+")
    gather_d("c", xc, "x-")
    gather_d("c", xc, "y+")
    weights_end(1, 4)
    gather_d("c", xc, "y-")
    panels(forward, 7, 8)
    weights_far(2)
    turn_some(0, 16)
    weights_end(2, 4)
    panels(spread_out, 0, 2)
    panels(spread_out, 2, 4)
    panels(spread_out, 4, 6)
    panels(spread_out, 6, 8)
    collect(b_out, s_out, T_LAST_OUT)
    o_y1[0]()
    o_x1[0]()
    turn_some(16, 32)
    gather_end("c")
    panels(deltas, 0, 2)
    panels(deltas, 2, 4)
    panels(deltas, 4, 6)
    panels(deltas, 6, 8)
    panels(terms, 0, 1)
    sibling(4)
    panels(terms, 1, 3)
    sibling(3)
    sibling(-3)
    panels(backward, 0, 2)
    pair_sum(4)
    z_send("z+", 1, 0)
    z_send("z-", 1, 1)
    pair_sum(3)
    z_send("z+", 2, 1)
    pair_sum(-3)
    z_send("z-", 2, 0)
    o_y1[1]("+", 0)
    o_y1[1]("-", 0)
    o_x1[1]("+", 0)
    o_x1[1]("-", 0)
    panels(backward, 2, 4)
    panels(backward, 4, 6)
    panels(backward, 6, 8)
    collect(b_in, s_in, T_LAST_IN)
    i_y1[0]()
    i_x1[0]()
    panels(terms, 3, 5)
    sibling(2)
    sibling(-2)
    z_send("z+", 2, 0)
    z_send("z-", 2, 1)
    panels(terms, 5, 7)
    sibling(1)
    sibling(-1)
    pair_sum(2)
    z_send("z+", 3, 1)
    pair_sum(-2)
    z_send("z-", 3, 0)
    i_y1[1]("+", 0)
    pair_sum(1)
    pair_sum(-1)
    i_y1[1]("-", 0)
    i_x1[1]("+", 0)
    i_x1[1]("-", 0)
    o_y1[2](0)
    i_y1[1]("+", 1)
    i_y1[1]("-", 1)
    i_x1[1]("+", 1)
    i_x1[1]("-", 1)
    o_x2[0](0)
    o_x2[0](1)
    o_x1[2](0)
    o_y2[0](0)
    o_y2[0](1)
    z_send("z+", 3, 0)
    z_send("z-", 3, 1)
    panels(terms, 7, 8)
    sibling(0)
    z_send("z+", 4, 1)
    z_send("z-", 4, 0)
    pair_sum(0)
    i_y1[2](0)
    i_x2[0](0)
    i_x1[2](0)
    i_y2[0](0)
    i_y1[2](1)
    i_x2[0](1)
    i_x1[2](1)
    i_y2[0](1)
    z_send("z+", 4, 0)
    z_send("z-", 4, 1)
    o_y2[1]()
    o_x2[1]()
    write_out(out_ref, b_out)
    i_y2[1]()
    i_x2[1]()
    write_out(in_ref, b_in)
    z_last(0)
    z_last(1)
    cp.recv(("gf", 0))
    cp.recv(("gf", 1))
    cp.finish()


def finish(out, in_grad, grads, out_, in_grad_, gate, up, down, sems):
    pairs = [(out, out_), (in_grad, in_grad_)]
    pairs += [(grads.at[i], ref.at[0]) for i, ref in enumerate((gate, up, down))]
    copies = [pltpu.make_async_copy(*pair, sems.at[i]) for i, pair in enumerate(pairs)]
    for copy in copies:
        copy.start()
    for copy in copies:
        copy.wait()


def per_device(
    tokens, cotangent, gate_blocks, up_blocks, down_blocks, gate_index, up_index, down_index
):
    hbm_spec = pl.BlockSpec(memory_space=pltpu.HBM)
    vmem_spec = pl.BlockSpec(memory_space=pltpu.VMEM)
    grad = jax.ShapeDtypeStruct((1, SLOTS, BLK, BLK), F32)
    act = jax.ShapeDtypeStruct((128, 4 * BLK), BF16)
    big = (4, 4, 2, 256, BLK)
    results = pl.pallas_call(
        kernel,
        out_shape=(act, act, jax.ShapeDtypeStruct((3, SLOTS, BLK, BLK), F32)),
        in_specs=[hbm_spec] * 8,
        out_specs=(vmem_spec,) * 3,
        scratch_shapes=[
            pltpu.VMEM((3, SLOTS, BLK), I32),
            pltpu.VMEM((T_ROWS, BLK), I32),
            pltpu.SMEM((T_ROWS, BLK), I32),
            pltpu.VMEM((5, 4, 2, 256, BLK), BF16),
            pltpu.VMEM((5, 4, 2, 256, BLK), BF16),
            pltpu.VMEM((5, 4, 2, BLK, 256), BF16),
            pltpu.VMEM((3, GROUP, SLOTS, BLK, BLK), BF16),
            pltpu.VMEM((NBLK + 1, 256, BLK), F32),
            pltpu.VMEM((2 * NBLK + 1, 256, BLK), F32),
            pltpu.VMEM((GROUP, 256, BLK), BF16),
            pltpu.VMEM((GROUP, 256, BLK), BF16),
            pltpu.VMEM((GROUP, 256, BLK), BF16),
            pltpu.VMEM((GROUP, 256, BLK), F32),
            pltpu.VMEM((GROUP, 256, BLK), F32),
            pltpu.VMEM(big, BF16),
            pltpu.VMEM(big, BF16),
            pltpu.VMEM((3, GROUP, SLOTS, BLK, BLK), BF16),
            pltpu.VMEM((2, 3, 2, 2, 256, BLK), BF16),
            pltpu.VMEM((2, 3, 2, 4, 128, BLK), BF16),
            pltpu.VMEM((2, 3, 2, 128, BLK), BF16),
            pltpu.VMEM((2, 3, 2, 128, BLK), BF16),
            pltpu.VMEM((3, GROUP, 2, BLK, BLK), BF16),
            pltpu.VMEM((2, 4, 2, 3, BLK, BLK), BF16),
            pltpu.SemaphoreType.DMA((1,)),
            pltpu.SemaphoreType.DMA((14,)),
            pltpu.SemaphoreType.DMA((SENDS,)),
            pltpu.SemaphoreType.DMA((RECVS,)),
        ],
        compiler_params=pltpu.CompilerParams(
            collective_id=0, has_side_effects=True, vmem_limit_bytes=60 << 20
        ),
        name="ffn",
    )(gate_index.T, up_index.T, down_index.T, tokens, cotangent, gate_blocks, up_blocks, down_blocks)
    return pl.pallas_call(
        finish,
        out_shape=(act, act, grad, grad, grad),
        in_specs=[vmem_spec] * 3,
        out_specs=(hbm_spec,) * 5,
        scratch_shapes=[pltpu.SemaphoreType.DMA((5,))],
        name="results",
    )(*results)


def solution(mesh):
    act = P(("dp", "col"), "row")
    blocks = P(("row", "col"), None, None, None)
    return jax.shard_map(
        per_device,
        mesh=mesh,
        in_specs=(act, act, blocks, blocks, blocks, P(), P(), P()),
        out_specs=(act, act, blocks, blocks, blocks),
        check_vma=False,
    )
```

```python
import jax
import jax.numpy as jnp
from jax import lax
from jax.experimental import pallas as pl
from jax.experimental.pallas import tpu as pltpu
from jax.sharding import PartitionSpec as P

BLK = 128
SLOTS = 4
GROUP = 8
NBLK = 32
SENDS, RECVS = 40, 77
F32 = jnp.float32
BF16 = jnp.bfloat16
MESH = pl.DeviceIdType.MESH

T_GATE, T_UP, T_DOWN, T_PREV_OUT, T_PREV_GATE, T_PREV_UP, T_LAST_OUT, T_LAST_IN = 0, 4, 8, 12, 16, 20, 24, 56
T_ROWS = 88
I32 = jnp.int32


def dot(a, b, dims):
    return lax.dot_general(a, b, (dims, ((), ())), preferred_element_type=F32)


def block_of(ref, place):
    return ref[place // 8, (place // 2) % 4, place % 2]


class Copies:
    def __init__(self, send_sem, recv_sem, neighbours, back):
        self.send_sem, self.recv_sem, self.neighbours, self.back = send_sem, recv_sem, neighbours, back
        self.made, self.used, self.clock, self.recv_count = {}, [], 0, 0

    def free(self, way):
        heard = max(
            (m["sent"] for m in self.made.values() if m["way"] == self.back.get(way, way) and m["got"]),
            default=-1,
        )
        for m in self.made.values():
            if m["way"] == way and m["held"] and m["got"] and m["got"] < heard:
                m["held"] = False
                return m["number"]
        self.recv_count += 1
        return self.recv_count - 1

    def send(self, name, src, dst, way):
        self.clock += 1
        number = self.free(way)
        if len(self.used) < SENDS:
            slot = len(self.used)
        else:
            slot, earlier = self.used[-SENDS]
            earlier.wait_send()
        copy = pltpu.make_async_remote_copy(
            src_ref=src,
            dst_ref=dst,
            send_sem=self.send_sem.at[slot],
            recv_sem=self.recv_sem.at[number],
            device_id=self.neighbours[way],
            device_id_type=MESH,
        )
        copy.start()
        self.used.append((slot, copy))
        self.made[name] = {
            "copy": copy, "way": way, "number": number, "sent": self.clock, "got": 0, "held": True,
        }

    def recv(self, name):
        self.clock += 1
        self.made[name]["copy"].wait_recv()
        self.made[name]["got"] = self.clock

    def finish(self):
        assert self.recv_count <= RECVS, self.recv_count
        for _, copy in self.used[-SENDS:]:
            copy.wait_send()


def add_into(dst, srcs, dims, rows=64):
    total = 1
    for size in dims[:-2]:
        total *= size
    per = dims[-2] // rows

    def body(i, _):
        index = []
        rest = i // per
        for size in reversed(dims[:-2]):
            index.insert(0, rest % size)
            rest = rest // size
        index = tuple(index) + (pl.ds(pl.multiple_of((i % per) * rows, rows), rows),)
        value = dst[index].astype(F32)
        for src in srcs:
            value = value + src[index].astype(F32)
        dst[index] = value.astype(dst.dtype)
        return 0

    lax.fori_loop(0, total * per, body, 0, unroll=2)


def make_table(keys, tab, first):
    lane = lax.broadcasted_iota(I32, (SLOTS, BLK), 1)
    panel = lane & 7

    def place(v):
        return jnp.where(v < NBLK, (v & 3) * 8 + (v >> 2), NBLK)

    gate, up, down = (place(keys[i]) for i in range(3))
    tab[T_GATE:T_GATE + SLOTS] = gate
    tab[T_UP:T_UP + SLOTS] = up
    tab[T_DOWN:T_DOWN + SLOTS] = down

    prev_out = jnp.full((SLOTS, BLK), NBLK, I32)
    prev_gate = jnp.full((SLOTS, BLK), 2 * NBLK, I32)
    prev_up = prev_gate
    for d in range(GROUP - 1, -1, -1):
        far = panel >= d
        if d:
            moved = pltpu.roll(down, d, axis=1)
            for s in range(SLOTS):
                hit = (down == moved[s:s + 1]) & far
                prev_out = jnp.where(hit, (panel - d) * SLOTS + s, prev_out)
        for i, src in enumerate((gate, up)):
            if d == 0 and i == 1:
                continue
            moved = pltpu.roll(src, d, axis=1) if d else src
            for s in range(SLOTS):
                number = (panel - d) * 8 + i * SLOTS + s
                if d:
                    prev_gate = jnp.where((gate == moved[s:s + 1]) & far, number, prev_gate)
                prev_up = jnp.where((up == moved[s:s + 1]) & far, number, prev_up)
    tab[T_PREV_OUT:T_PREV_OUT + SLOTS] = prev_out
    tab[T_PREV_GATE:T_PREV_GATE + SLOTS] = prev_gate
    tab[T_PREV_UP:T_PREV_UP + SLOTS] = prev_up

    wanted = lax.broadcasted_iota(I32, (NBLK, BLK), 0)
    ours = lax.broadcasted_iota(I32, (NBLK, BLK), 1) - first
    inside = (ours >= 0) & (ours < GROUP)

    def last(sources, per):
        best = jnp.full((NBLK, BLK), -1, I32)
        for i, src in enumerate(sources):
            for s in range(SLOTS):
                hit = (wanted == src[s:s + 1]) & inside
                best = jnp.maximum(best, jnp.where(hit, ours * per + i * SLOTS + s, -1))
        best = jnp.max(best, axis=1, keepdims=True)
        best = jnp.where(best < 0, per * GROUP, best)
        return jnp.broadcast_to(best, (NBLK, BLK))

    tab[T_LAST_OUT:T_LAST_OUT + NBLK] = last((down,), SLOTS)
    tab[T_LAST_IN:T_LAST_IN + NBLK] = last((gate, up), 2 * SLOTS)


def kernel(
    gate_index, up_index, down_index, tokens, cotangent, gate_blocks, up_blocks, down_blocks,
    out_hbm, in_hbm, grad_hbm,
    out_ref, in_ref, grad_ref,
    keys, tab, table, xt, xc, turned, w, s_out, s_in, act_s, gd_s, ud_s, swish_s, slope_s,
    b_out, b_in, grads, ra, rb, qa, qb, g_sib, rz,
    key_sem, local_sem, out_sem, send_sem, recv_sem,
):
    core = lax.axis_index("dp")
    row = lax.axis_index("row")
    col = lax.axis_index("col")
    y, xh, xl, z = row // 2, row % 2, col // 8, col % 8
    x = xh * 2 + xl

    def at(core=core, x=x, y=y, z=z):
        return (core, y * 2 + x // 2, (x % 2) * 8 + z)

    xs = [(x + o) % 4 for o in range(4)]
    ys = [(y + o) % 4 for o in range(4)]
    zs = [(z + o) % 8 for o in range(8)]
    ways = {
        "x+": at(x=xs[1]), "x-": at(x=xs[3]), "y+": at(y=ys[1]), "y-": at(y=ys[3]),
        "z+": at(z=zs[1]), "z-": at(z=zs[7]), "c": at(core=1 - core),
    }
    yp, yl = y // 2, y % 2
    met = list(ways.values()) + [at(x=xs[2]), at(y=ys[2])]
    ways.update({
        ("x", 0): at(x=(1 - xh) * 2 + xl), ("x", 1): at(x=(1 - xh) * 2 + 1 - xl),
        ("x", 2): at(x=xh * 2 + 1 - xl), ("y", 0): at(y=(1 - yp) * 2 + yl),
        ("y", 1): at(y=(1 - yp) * 2 + 1 - yl), ("y", 2): at(y=yp * 2 + 1 - yl),
    })
    back = {"x+": "x-", "x-": "x+", "y+": "y-", "y-": "y+", "z+": "z-", "z-": "z+"}
    cp = Copies(send_sem, recv_sem, ways, back)

    barrier = pltpu.get_barrier_semaphore()
    for device in met:
        pl.semaphore_signal(barrier, inc=1, device_id=device, device_id_type=MESH)

    def half(x_):
        return pl.ds(pl.multiple_of((x_ % 2) * 128, 128), 128)

    local = {}

    def copy_in(name, src, dst):
        copy = pltpu.make_async_copy(src, dst, local_sem.at[len(local)])
        copy.start()
        local[name] = copy

    for t, src, dst in (("t", tokens, xt), ("c", cotangent, xc)):
        for hj in range(4):
            copy_in((t, hj), src.at[:, pl.ds(hj * BLK, BLK)], dst.at[hj, y, xh, half(x)])
    for i, src in enumerate((gate_blocks, up_blocks, down_blocks)):
        copy_in(("w", i), src.at[0], w.at[i, z])
    for i, src in enumerate((gate_index, up_index, down_index)):
        copy_in(("k", i), src, keys.at[i])
    pl.semaphore_wait(barrier, len(met))

    def landed(name, count):
        for i in range(count):
            local[name, i].wait()

    def piece(ref, hj, n, y_, x_):
        return ref.at[pl.ds(hj, n), y_, x_ // 2, half(x_)]

    def line_x(ref, hj, y_):
        return ref.at[hj, y_]

    def line_y(ref, hj, x_):
        return ref.at[hj, :, x_ // 2, half(x_)]

    def send_same(name, ref, way):
        cp.send(name, ref, ref, way)

    def gather_a(t, ref, src):
        for hj, way in ((0, "x+"), (1, "x-"), (2, "y+"), (3, "y-"), (1, "x+"), (0, "x-"), (3, "y+"), (2, "y-")):
            cp.send(
                (t, "a", way, hj), src.at[:, pl.ds(hj * BLK, BLK)], ref.at[hj, y, xh, half(x)], way
            )

    def gather_b(t, ref, way):
        hj, y_, x_ = {
            "x+": (0, y, xs[3]), "x-": (1, y, xs[1]), "y+": (2, ys[3], x), "y-": (3, ys[1], x),
        }[way]
        cp.recv((t, "a", way, hj))
        send_same((t, "b", way), piece(ref, hj, 1, y_, x_), way)

    def gather_c1(t, ref):
        cp.recv((t, "a", "x+", 1))
        cp.recv((t, "a", "x-", 0))
        cp.recv((t, "b", "x+"))
        cp.recv((t, "b", "x-"))
        for hj, way in ((0, "y+"), (1, "y-"), (1, "y+"), (0, "y-")):
            send_same((t, "c", way, hj), line_x(ref, hj, y), way)

    def gather_c2(t, ref):
        cp.recv((t, "a", "y+", 3))
        cp.recv((t, "a", "y-", 2))
        cp.recv((t, "b", "y+"))
        cp.recv((t, "b", "y-"))
        for hj, way in ((2, "x+"), (3, "x-"), (3, "x+"), (2, "x-")):
            send_same((t, "c", way, hj), line_y(ref, hj, x), way)

    def gather_d(t, ref, way):
        hj = {"y+": 0, "y-": 1, "x+": 2, "x-": 3}[way]
        cp.recv((t, "c", way, hj))
        part = {
            "y+": line_x(ref, 0, ys[3]), "y-": line_x(ref, 1, ys[1]),
            "x+": line_y(ref, 2, xs[3]), "x-": line_y(ref, 3, xs[1]),
        }[way]
        send_same((t, "d", way), part, way)

    def gather_end(t):
        for hj, way in ((1, "y+"), (0, "y-"), (3, "x+"), (2, "x-")):
            cp.recv((t, "c", way, hj))
        for way in ("y+", "y-", "x+", "x-"):
            cp.recv((t, "d", way))

    mine = core * 2

    def w_piece(i, o, first=0, n=2):
        return w.at[i, zs[o % 8], pl.ds(mine + first, n)]

    def weights_first(i):
        src = (gate_blocks, up_blocks, down_blocks)[i].at[0, pl.ds(mine, 2)]
        for way in ("z+", "z-"):
            cp.send(("w", i, 1, way), src, w_piece(i, 0), way)

    def weights_step(i, k, way):
        o, first = (-k, 0) if way == "z+" else (k, 1)
        cp.recv(("w", i, k, way))
        if k < 3:
            send_same(("w", i, k + 1, way), w_piece(i, o), way)
        else:
            send_same(("w", i, 4, way), w_piece(i, o, first, 1), way)
        send_same(("ws", i, -o), w_piece(i, o), "c")

    def weights_far(i):
        cp.recv(("w", i, 4, "z+"))
        cp.recv(("w", i, 4, "z-"))
        send_same(("ws", i, 4), w_piece(i, 4), "c")

    def weights_end(i, k):
        cp.recv(("ws", i, k))
        if k < 4:
            cp.recv(("ws", i, -k))

    line = (row * 2 + xl) * GROUP
    def picked(ref, first, p, axis=1):
        return jnp.concatenate(
            [block_of(ref, table[first + s, line + p]) for s in range(SLOTS)], axis=axis
        )

    def w_rows(i, p):
        return w[i, p].reshape(SLOTS * BLK, BLK)

    def w_lanes(i, p):
        return jnp.concatenate([w[i, p, s] for s in range(SLOTS)], axis=1)

    def forward(j, _):
        p = (z + 8 + ((j + 1) // 2) * (2 * (j % 2) - 1)) % GROUP
        gate = dot(picked(xt, T_GATE, p), w_rows(0, p), ((1,), (0,)))
        up = dot(picked(xt, T_UP, p), w_rows(1, p), ((1,), (0,)))
        sig = jax.nn.sigmoid(gate)
        swish = gate * sig
        act = (swish * up).astype(BF16)
        act_s[p] = act
        swish_s[p] = swish
        slope_s[p] = up * (sig * (1.0 + gate * (1.0 - sig)))
        return 0

    def spread_out(p, _):
        before = [s_out[table[T_PREV_OUT + s, line + p]] for s in range(SLOTS)]
        spread = dot(act_s[p], w_lanes(2, p), ((1,), (0,)))
        for s in range(SLOTS):
            s_out[p * SLOTS + s] = before[s] + spread[:, s * BLK:(s + 1) * BLK]
        return 0

    def deltas(p, _):
        act_grad = dot(picked(xc, T_DOWN, p), w_lanes(2, p), ((1,), (1,)))
        gd_s[p] = (act_grad * slope_s[p]).astype(BF16)
        ud_s[p] = (act_grad * swish_s[p]).astype(BF16)
        return 0

    def backward(p, _):
        for i, delta, first in ((0, gd_s, T_PREV_GATE), (1, ud_s, T_PREV_UP)):
            before = [s_in[table[first + s, line + p]] for s in range(SLOTS)]
            back = dot(delta[p], w_rows(i, p), ((1,), (1,)))
            for s in range(SLOTS):
                s_in[p * 8 + i * SLOTS + s] = before[s] + back[:, s * BLK:(s + 1) * BLK]
        return 0

    def terms(j, _):
        odd = j % 2
        p = (z + 4 + (j // 2) * (1 - odd) - ((j + 1) // 2) * odd) % GROUP
        term = dot(act_s[p], picked(xc, T_DOWN, p), ((0,), (0,)))
        for s in range(SLOTS):
            grads[2, p, s] = term[:, s * BLK:(s + 1) * BLK].astype(BF16)
        for i, first, delta in ((0, T_GATE, gd_s), (1, T_UP, ud_s)):
            term = dot(picked(turned, first, p, axis=0), delta[p], ((1,), (0,)))
            grads[i, p] = term.astype(BF16).reshape(SLOTS, BLK, BLK)
        return 0

    def turn(q, _):
        turned[q // 8, (q // 2) % 4, q % 2] = xt[q // 8, (q // 2) % 4, q % 2].T
        return 0

    def panels(body, lower=0, upper=GROUP):
        lax.fori_loop(lower, upper, body, 0, unroll=upper - lower)

    def collect(dst, src, first):
        def body(q, _):
            dst[q // 8, (q // 2) % 4, q % 2] = src[table[first + q, 0]].astype(BF16)
            return 0

        lax.fori_loop(0, NBLK, body, 0, unroll=4)

    def stage(t, name, axis, hj, part, bufs, cut, dims, halves):
        near = xs if axis == "x" else ys
        plus, minus = axis + "+", axis + "-"
        b1, b2, b3 = bufs

        def first():
            for n, far, mid in ((1, 2, (0, 1)), (2, 0, (1, 0))):
                for h in range(halves):
                    for d, way in enumerate((plus, minus)):
                        there = near[2] if n == 1 else near[(1, 3)[d]]
                        buf = (b1, b2)[n - 1].at[d]
                        cp.send((t, name, n, way, h), cut(part(hj + mid[d], there), h), cut(buf, h), way)

        def second(sign, h):
            way, part_, d = (
                (plus, part(hj, near[1]), 0) if sign == "+" else (minus, part(hj + 1, near[3]), 1)
            )
            cp.recv((t, name, 1, way, h))
            add_into(cut(part_, h), [cut(b1.at[d], h)], dims)
            cp.send((t, name, 3, way, h), cut(part_, h), cut(b3.at[d], h), way)

        def third(h):
            cp.recv((t, name, 2, plus, h))
            cp.recv((t, name, 2, minus, h))
            cp.recv((t, name, 3, plus, h))
            add_into(cut(part(hj, near[0]), h), [cut(b3.at[0], h), cut(b2.at[1], h)], dims)
            cp.recv((t, name, 3, minus, h))
            add_into(cut(part(hj + 1, near[0]), h), [cut(b2.at[0], h), cut(b3.at[1], h)], dims)

        return first, second, third

    def direct(t, name, axis, part, buf):
        def first(h):
            for n in ((0, 1), (2,))[h]:
                cp.send((t, name, n), part(n), buf.at[n], (axis, n))

        def last():
            for n in range(3):
                cp.recv((t, name, n))
            add_into(part(3), [buf.at[n] for n in range(3)], (2, 128, BLK))

        return first, last

    def reduce_of(k, t, ref):
        def along_x(hj, y_):
            return ref.at[hj, y_]

        def along_y(hj, x_):
            return ref.at[hj, :, x_ // 2, half(x_)]

        def end_x(n):
            xh_, xl_ = (1 - xh if n < 2 else xh), (xl if n in (0, 3) else 1 - xl)
            return ref.at[pl.ds(0, 2), y, xh_, half(xl_)]

        def end_y(n):
            yp_, yl_ = (1 - yp if n < 2 else yp), (yl if n in (0, 3) else 1 - yl)
            return ref.at[pl.ds(2, 2), yp_ * 2 + yl_, xh, half(x)]

        halves = 1 + k

        def cut_x(part, h):
            return part.at[xh if h else 1 - xh] if k else part

        def cut_y(part, h):
            return part.at[pl.ds((yp if h else 1 - yp) * 2, 2)] if k else part

        dims = ((2, 256, BLK), (4, 128, BLK)) if k == 0 else ((256, BLK), (2, 128, BLK))

        y1 = stage(t, "y1", "y", 0, along_x, [ra.at[k, i] for i in range(3)], cut_x, dims[0], halves)
        x1 = stage(t, "x1", "x", 2, along_y, [rb.at[k, i] for i in range(3)], cut_y, dims[1], halves)
        x2 = direct(t, "x2", "x", end_x, qa.at[k])
        y2 = direct(t, "y2", "y", end_y, qb.at[k])
        return y1, x1, x2, y2

    o_y1, o_x1, o_x2, o_y2 = reduce_of(0, "o", b_out)
    i_y1, i_x1, i_x2, i_y2 = reduce_of(1, "i", b_in)

    theirs = (1 - core) * 2

    def sibling(o):
        p = zs[o % 8]
        cp.send(("gs", o), grads.at[:, p, pl.ds(theirs, 2)], g_sib.at[:, p], "c")

    def pair_sum(o):
        cp.recv(("gs", o))
        p = zs[o % 8]
        add_into(grads.at[:, p, pl.ds(mine, 2)], [g_sib.at[:, p]], (3, 2, 128, BLK))

    def z_send(way, k, s):
        d, sign, begins = (0, 1, 0) if way == "z+" else (1, -1, 1)
        for i, n in ((2, 1), (0, 2)):
            part = grads.at[pl.ds(i, n), zs[sign * (5 - k) % 8], mine + s]
            if k > 2 or (k == 2 and s == begins):
                cp.recv(("z", way, k - 1, s, i))
                add_into(part, [rz.at[d, k - 2, s, pl.ds(i, n)]], (n, 128, BLK))
            cp.send(("z", way, k, s, i), part, rz.at[d, k - 1, s, pl.ds(i, n)], way)

    def z_last(s):
        for i in (2, 0):
            cp.recv(("z", "z+", 4, s, i))
            cp.recv(("z", "z-", 4, s, i))

        def body(n, _):
            rows = pl.ds(pl.multiple_of((n % 2) * 64, 64), 64)
            i = n // 2
            grad_ref[i, mine + s, rows] = (
                grads[i, z, mine + s, rows].astype(F32)
                + rz[0, 3, s, i, rows].astype(F32)
                + rz[1, 3, s, i, rows].astype(F32)
            )
            return 0

        lax.fori_loop(0, 6, body, 0)
        part = grad_ref.at[:, mine + s]
        cp.send(("gf", s), part, part, "c")

    table_copy = pltpu.make_async_copy(tab, table, key_sem.at[0])

    def table_start():
        landed("k", 3)
        make_table(keys, tab, line)
        table_copy.start()

    def zeros():
        for ref in (xt, xc):
            ref[4, 0, 0] = jnp.zeros((256, BLK), BF16)
        turned[4, 0, 0] = jnp.zeros((BLK, 256), BF16)
        s_out[NBLK] = jnp.zeros((256, BLK), F32)
        s_in[2 * NBLK] = jnp.zeros((256, BLK), F32)

    def turn_some(lower, upper):
        lax.fori_loop(lower, upper, turn, 0, unroll=4)

    out_copy, in_copy, grad_copy = (
        pltpu.make_async_copy(src, dst, out_sem.at[n])
        for n, (src, dst) in enumerate(((out_ref, out_hbm), (in_ref, in_hbm), (grad_ref, grad_hbm)))
    )

    def write_out(ref, b):
        for hj in range(4):
            ref[:, hj * BLK:(hj + 1) * BLK] = b[hj, y, xh, half(x)]
        (out_copy if ref is out_ref else in_copy).start()

    gather_a("t", xt, tokens)
    weights_first(0)
    weights_first(1)
    gather_a("c", xc, cotangent)
    weights_first(2)
    table_start()
    landed("t", 4)
    landed("w", 3)
    landed("c", 4)
    table_copy.wait()
    zeros()
    gather_b("t", xt, "x+")
    gather_b("t", xt, "x-")
    gather_b("t", xt, "y+")
    gather_b("t", xt, "y-")
    gather_b("c", xc, "x+")
    gather_b("c", xc, "x-")
    gather_b("c", xc, "y+")
    gather_b("c", xc, "y-")
    weights_step(0, 1, "z+")
    weights_step(0, 1, "z-")
    weights_end(0, 1)
    weights_step(1, 1, "z+")
    weights_step(1, 1, "z-")
    gather_c1("t", xt)
    gather_c2("t", xt)
    weights_end(1, 1)
    weights_step(2, 1, "z+")
    weights_step(2, 1, "z-")
    weights_end(2, 1)
    weights_step(0, 2, "z+")
    weights_step(0, 2, "z-")
    weights_end(0, 2)
    weights_step(1, 2, "z+")
    weights_step(1, 2, "z-")
    weights_end(1, 2)
    gather_d("t", xt, "y+")
    gather_d("t", xt, "y-")
    weights_step(2, 2, "z+")
    weights_step(2, 2, "z-")
    gather_d("t", xt, "x+")
    gather_d("t", xt, "x-")
    gather_c1("c", xc)
    gather_c2("c", xc)
    weights_end(2, 2)
    weights_step(0, 3, "z+")
    weights_step(0, 3, "z-")
    weights_end(0, 3)
    weights_step(1, 3, "z+")
    weights_step(1, 3, "z-")
    weights_end(1, 3)
    weights_step(2, 3, "z+")
    weights_step(2, 3, "z-")
    gather_end("t")
    weights_end(2, 3)
    panels(forward, 0, 1)
    weights_far(0)
    panels(forward, 1, 3)
    panels(forward, 3, 5)
    weights_far(1)
    weights_end(0, 4)
    panels(forward, 5, 7)
    gather_d("c", xc, "x+")
    gather_d("c", xc, "x-")
    gather_d("c", xc, "y+")
    weights_end(1, 4)
    gather_d("c", xc, "y-")
    panels(forward, 7, 8)
    weights_far(2)
    turn_some(0, 16)
    weights_end(2, 4)
    panels(spread_out, 0, 2)
    panels(spread_out, 2, 4)
    panels(spread_out, 4, 6)
    panels(spread_out, 6, 8)
    collect(b_out, s_out, T_LAST_OUT)
    o_y1[0]()
    o_x1[0]()
    turn_some(16, 32)
    gather_end("c")
    panels(deltas, 0, 2)
    panels(deltas, 2, 4)
    panels(deltas, 4, 6)
    panels(deltas, 6, 8)
    panels(terms, 0, 1)
    sibling(4)
    panels(terms, 1, 3)
    sibling(3)
    sibling(-3)
    panels(backward, 0, 2)
    pair_sum(4)
    z_send("z+", 1, 0)
    z_send("z-", 1, 1)
    pair_sum(3)
    z_send("z+", 2, 1)
    pair_sum(-3)
    z_send("z-", 2, 0)
    o_y1[1]("+", 0)
    o_y1[1]("-", 0)
    o_x1[1]("+", 0)
    o_x1[1]("-", 0)
    panels(backward, 2, 4)
    panels(backward, 4, 6)
    panels(backward, 6, 8)
    collect(b_in, s_in, T_LAST_IN)
    i_y1[0]()
    i_x1[0]()
    panels(terms, 3, 5)
    sibling(2)
    sibling(-2)
    z_send("z+", 2, 0)
    z_send("z-", 2, 1)
    panels(terms, 5, 7)
    sibling(1)
    sibling(-1)
    pair_sum(2)
    z_send("z+", 3, 1)
    pair_sum(-2)
    z_send("z-", 3, 0)
    i_y1[1]("+", 0)
    pair_sum(1)
    pair_sum(-1)
    i_y1[1]("-", 0)
    i_x1[1]("+", 0)
    i_x1[1]("-", 0)
    o_y1[2](0)
    i_y1[1]("+", 1)
    i_y1[1]("-", 1)
    i_x1[1]("+", 1)
    i_x1[1]("-", 1)
    o_x2[0](0)
    o_x2[0](1)
    o_x1[2](0)
    o_y2[0](0)
    o_y2[0](1)
    z_send("z+", 3, 0)
    z_send("z-", 3, 1)
    panels(terms, 7, 8)
    sibling(0)
    z_send("z+", 4, 1)
    z_send("z-", 4, 0)
    pair_sum(0)
    i_y1[2](0)
    i_x2[0](0)
    i_x1[2](0)
    i_y2[0](0)
    i_y1[2](1)
    i_x2[0](1)
    i_x1[2](1)
    i_y2[0](1)
    z_send("z+", 4, 0)
    z_send("z-", 4, 1)
    o_y2[1]()
    o_x2[1]()
    write_out(out_ref, b_out)
    i_y2[1]()
    i_x2[1]()
    write_out(in_ref, b_in)
    z_last(0)
    z_last(1)
    cp.recv(("gf", 0))
    cp.recv(("gf", 1))
    grad_copy.start()
    cp.finish()
    for copy in (out_copy, in_copy, grad_copy):
        copy.wait()


def finish(out, in_grad, grads, out_, in_grad_, gate, up, down, sems):
    pairs = [(out, out_), (in_grad, in_grad_)]
    pairs += [(grads.at[i], ref.at[0]) for i, ref in enumerate((gate, up, down))]
    copies = [pltpu.make_async_copy(*pair, sems.at[i]) for i, pair in enumerate(pairs)]
    for copy in copies:
        copy.start()
    for copy in copies:
        copy.wait()


def per_device(
    tokens, cotangent, gate_blocks, up_blocks, down_blocks, gate_index, up_index, down_index
):
    hbm_spec = pl.BlockSpec(memory_space=pltpu.HBM)
    vmem_spec = pl.BlockSpec(memory_space=pltpu.VMEM)
    grad = jax.ShapeDtypeStruct((1, SLOTS, BLK, BLK), F32)
    act = jax.ShapeDtypeStruct((128, 4 * BLK), BF16)
    big = (4, 4, 2, 256, BLK)
    results = pl.pallas_call(
        kernel,
        out_shape=(act, act, jax.ShapeDtypeStruct((3, SLOTS, BLK, BLK), F32)),
        in_specs=[hbm_spec] * 8,
        out_specs=(hbm_spec,) * 3,
        scratch_shapes=[
            pltpu.VMEM((128, 4 * BLK), BF16),
            pltpu.VMEM((128, 4 * BLK), BF16),
            pltpu.VMEM((3, SLOTS, BLK, BLK), F32),
            pltpu.VMEM((3, SLOTS, BLK), I32),
            pltpu.VMEM((T_ROWS, BLK), I32),
            pltpu.SMEM((T_ROWS, BLK), I32),
            pltpu.VMEM((5, 4, 2, 256, BLK), BF16),
            pltpu.VMEM((5, 4, 2, 256, BLK), BF16),
            pltpu.VMEM((5, 4, 2, BLK, 256), BF16),
            pltpu.VMEM((3, GROUP, SLOTS, BLK, BLK), BF16),
            pltpu.VMEM((NBLK + 1, 256, BLK), F32),
            pltpu.VMEM((2 * NBLK + 1, 256, BLK), F32),
            pltpu.VMEM((GROUP, 256, BLK), BF16),
            pltpu.VMEM((GROUP, 256, BLK), BF16),
            pltpu.VMEM((GROUP, 256, BLK), BF16),
            pltpu.VMEM((GROUP, 256, BLK), F32),
            pltpu.VMEM((GROUP, 256, BLK), F32),
            pltpu.VMEM(big, BF16),
            pltpu.VMEM(big, BF16),
            pltpu.VMEM((3, GROUP, SLOTS, BLK, BLK), BF16),
            pltpu.VMEM((2, 3, 2, 2, 256, BLK), BF16),
            pltpu.VMEM((2, 3, 2, 4, 128, BLK), BF16),
            pltpu.VMEM((2, 3, 2, 128, BLK), BF16),
            pltpu.VMEM((2, 3, 2, 128, BLK), BF16),
            pltpu.VMEM((3, GROUP, 2, BLK, BLK), BF16),
            pltpu.VMEM((2, 4, 2, 3, BLK, BLK), BF16),
            pltpu.SemaphoreType.DMA((1,)),
            pltpu.SemaphoreType.DMA((14,)),
            pltpu.SemaphoreType.DMA((3,)),
            pltpu.SemaphoreType.DMA((SENDS,)),
            pltpu.SemaphoreType.DMA((RECVS,)),
        ],
        compiler_params=pltpu.CompilerParams(
            collective_id=0, has_side_effects=True, vmem_limit_bytes=60 << 20
        ),
        name="ffn",
    )(gate_index.T, up_index.T, down_index.T, tokens, cotangent, gate_blocks, up_blocks, down_blocks)
    return pl.pallas_call(
        finish,
        out_shape=(act, act, grad, grad, grad),
        in_specs=[vmem_spec] * 3,
        out_specs=(hbm_spec,) * 5,
        scratch_shapes=[pltpu.SemaphoreType.DMA((5,))],
        name="results",
    )(*results)


def solution(mesh):
    act = P(("dp", "col"), "row")
    blocks = P(("row", "col"), None, None, None)
    return jax.shard_map(
        per_device,
        mesh=mesh,
        in_specs=(act, act, blocks, blocks, blocks, P(), P(), P()),
        out_specs=(act, act, blocks, blocks, blocks),
        check_vma=False,
    )
```
